512 devices in a mesh: azi: 64 (over y, z_lo, core), rad: 2 (over z_hi), batch: 4 (over x).
Axes of the slice: x: 4, y: 8, z: 8 (z_hi: 2, z_lo: 4; z = z_hi * 4 + z_lo), core: 2. Of those that a mesh axis runs over, the one named last changes fastest.
Arguments:
- snapshots: bfloat16 [4, 1024, 256, 256], P('batch', 'azi', 'rad'), may hold values from -6 to 6
- first_kernel: bfloat16 [9, 256, 256], P(None, None, 'batch'), may hold values from -0.125 to 0.125
- second_kernel: bfloat16 [9, 256, 256], P(None, None, 'batch'), may hold values from -0.125 to 0.125
- cotangent: bfloat16 [4, 512, 128, 256], P('batch', 'azi', 'rad'), may hold values from -16 to 16
Outputs:
- encoded: bfloat16 [4, 512, 128, 256], P('batch', 'azi', 'rad')
- input_grad: bfloat16 [4, 1024, 256, 256], P('batch', 'azi', 'rad')
- kernel_grad: float32 [589824], P(('azi', 'rad', 'batch'))
The draws below stay inside these ranges and needn't reach their ends.
All inputs are finite; a program needn't handle non-finite values.
Results may differ from the reference program's by a relative error of at most 0.0095.
Values may be sent and summed in bfloat16 or wider, within the bound.
A program may use at most 64 MiB of HBM per device.

```python
import math
import jax
import jax.numpy as jnp
from jax import lax

C = 256
TAPS = 9
BATCH = 4
NA = 1024
NR = 256


def spiked(result, stream_key, source, target, shards_of, factor):
    def block_of(axis_at):
        return (jnp.arange(result.shape[axis_at]) // (result.shape[axis_at] // shards_of)).reshape((-1,) + (1,) * (result.ndim - 1 - axis_at))

    first = jax.random.permutation(stream_key, shards_of)[block_of(target)]
    second = (block_of(target) + shards_of // 2) % shards_of
    return jnp.where((block_of(source) == first) | (block_of(source) == second), factor * result, result)


def block_levels(rng, extent, cuts, least, largest):
    loudness, own = 1.0, jax.random.fold_in(rng, 6)
    for position, shards_of in cuts:
        heights = jnp.exp(jax.random.uniform(jax.random.fold_in(own, position), (shards_of,), jnp.float32, least / len(cuts), largest / len(cuts)))
        loudness = loudness * jnp.repeat(heights, extent[position] // shards_of).reshape([-1 if axis == position else 1 for axis in range(len(extent))])
    return loudness


def normal_values(key, extent, spread, bound, cuts=(), kind=jnp.bfloat16):
    level = block_levels(key, extent, cuts, -0.22, 0.18) if cuts else 1.0
    drawn = jax.random.normal(key, extent, jnp.float32) * spread * level
    return jnp.minimum(jnp.maximum(drawn, -bound), bound).astype(kind)


def heavy_noise(rng, extent, spread, most, cuts, heavy, dtype=jnp.bfloat16):
    values = spread * jax.random.normal(rng, extent, jnp.float32)
    if cuts:
        values = values * block_levels(rng, extent, cuts, -0.22, 0.18)
    return jnp.clip(spiked(values, jax.random.fold_in(rng, 3), *heavy), -most, most).astype(dtype)


def setup_inputs(seed: int = 0) -> dict:
    key_list = jax.random.split(jax.random.key(seed), 5)
    snapshots = normal_values(key_list[0], (BATCH, NA, NR, C), 1.0, 6.0, ((0, 4), (1, 64), (2, 2)))
    first_kernel = normal_values(key_list[1], (TAPS, C, C), (TAPS * C) ** -0.5, 0.125, ((2, 4),))
    second_kernel = normal_values(key_list[2], (TAPS, C, C), (TAPS * C) ** -0.5, 0.125, ((2, 4),))
    cotangent = heavy_noise(key_list[3], (BATCH, NA // 2, NR // 2, C), 1.0, 16.0, ((0, 4), (1, 64), (2, 2)), (1, 3, 64, 4.0))
    return dict(snapshots=snapshots, first_kernel=first_kernel, second_kernel=second_kernel, cotangent=cotangent)


def silu_slope(pre_act):
    sigmoid = jax.nn.sigmoid(pre_act)
    return sigmoid * (1.0 + pre_act * (1.0 - sigmoid))

def tap_conv(extended, weights, taps, stride, rows_out, cols_out, transpose):
    channels = extended.shape[-1]
    summed = jnp.zeros((rows_out * cols_out, channels), jnp.float32)
    for row_at, col_at, tap in taps:
        window = extended[row_at:row_at + stride * rows_out:stride, col_at:col_at + stride * cols_out:stride, :]
        window = window.reshape(rows_out * cols_out, channels)
        kernel = weights[tap].T if transpose else weights[tap]
        summed = summed + jnp.dot(window, kernel, preferred_element_type=jnp.float32)
    return summed.reshape(rows_out, cols_out, channels)

def parity_grad(grad_next, first_full, rows_out, cols_out):
    parity_taps = ([(1, 0)], [(2, 0), (0, 1)])
    channels = grad_next.shape[-1]
    row_list = []
    for row_parity in (0, 1):
        col_list = []
        for col_parity in (0, 1):
            taps = [(row_shift, col_shift, 3 * m + n) for m, row_shift in parity_taps[row_parity] for n, col_shift in parity_taps[col_parity]]
            col_list.append(tap_conv(grad_next, first_full, taps, 1, rows_out, cols_out, True))
        row_list.append(jnp.stack(col_list, axis=2))
    stacked = jnp.stack(row_list, axis=1)
    return stacked.reshape(2 * rows_out, 2 * cols_out, channels)

def kernel_terms(act_ext, cot, rows_out, cols_out):
    channels = cot.shape[-1]
    flat_cot = cot.reshape(rows_out * cols_out, channels)
    terms = []
    for m in range(3):
        for n in range(3):
            window = act_ext[4 * m:4 * m + rows_out, 4 * n:4 * n + cols_out, :].reshape(rows_out * cols_out, channels)
            terms.append(lax.dot_general(window, flat_cot, (((0,), (0,)), ((), ())), preferred_element_type=jnp.float32))
    return jnp.stack(terms)

def stride_taps():
    return [(m, n, 3 * m + n) for m in range(3) for n in range(3)]

def ahead_taps():
    return [(4 * m, 4 * n, 3 * m + n) for m in range(3) for n in range(3)]

def back_taps():
    return [(8 - 4 * m, 8 - 4 * n, 3 * m + n) for m in range(3) for n in range(3)]

def dilate_pad(field):
    wrapped = jnp.pad(field, ((4, 4), (0, 0), (0, 0)), mode='wrap')
    return jnp.pad(wrapped, ((0, 0), (4, 4), (0, 0)))

def one_snapshot(field, first_kernel, second_kernel, cot):
    rows_out = field.shape[0] // 2
    cols_out = field.shape[1] // 2
    extended = jnp.pad(jnp.concatenate([field[-1:], field], 0), ((0, 0), (1, 0), (0, 0)))
    pre_act = tap_conv(extended, first_kernel, stride_taps(), 2, rows_out, cols_out, False)
    activation = jax.nn.silu(pre_act).astype(jnp.bfloat16)
    act_ext = dilate_pad(activation)
    mixed_out = tap_conv(act_ext, second_kernel, ahead_taps(), 1, rows_out, cols_out, False)
    encoded = (activation.astype(jnp.float32) + mixed_out).astype(jnp.bfloat16)
    grad_ext = dilate_pad(cot)
    grad_act = cot.astype(jnp.float32) + tap_conv(grad_ext, second_kernel, back_taps(), 1, rows_out, cols_out, True)
    grad_pre = (grad_act * silu_slope(pre_act)).astype(jnp.bfloat16)
    grad_next = jnp.pad(jnp.concatenate([grad_pre, grad_pre[:1]], 0), ((0, 0), (0, 1), (0, 0)))
    input_grad = parity_grad(grad_next, first_kernel, rows_out, cols_out).astype(jnp.bfloat16)
    return (encoded, input_grad, kernel_terms(act_ext, cot, rows_out, cols_out))

def reference(snapshots, first_kernel, second_kernel, cotangent):
    outs_list = []
    grads_list = []
    kernel_sum = jnp.zeros((TAPS, C, C), jnp.float32)
    for index in range(BATCH):
        encoded, input_grad, terms = one_snapshot(snapshots[index], first_kernel, second_kernel, cotangent[index])
        outs_list.append(encoded)
        grads_list.append(input_grad)
        kernel_sum = kernel_sum + terms
    grad_scale = 1.0 / math.sqrt(BATCH * (NA // 2) * (NR // 2))
    return (jnp.stack(outs_list), jnp.stack(grads_list), (kernel_sum * grad_scale).reshape(TAPS * C * C))
```

```python
import jax
import jax.numpy as jnp
from jax import lax
from jax.experimental import pallas as pl
from jax.experimental.pallas import tpu as pltpu
from jax.sharding import PartitionSpec as P

BF = jnp.bfloat16
F32 = jnp.float32
SHIFTS = (4, 0, -4)


def dot_nt(a, b):
    return lax.dot_general(a, b, (((1,), (1,)), ((), ())), preferred_element_type=F32)


def dot_nn(a, b):
    return lax.dot_general(a, b, (((1,), (0,)), ((), ())), preferred_element_type=F32)


def kernel(
    snap_hbm, w1_hbm, w2_hbm, cot_hbm,
    enc_ref, ing_ref, kg_ref,
    snap, xs, colf, cols_s, cols_r, w1, w2, cotr, cot_sh, edgef, cedge_s, cedge_r, aedge_s, aedge_r,
    extf, cot_h, actr, act_pair, act_sh, pre, at, gbuf, xbuf, xr, ysum, ybuf, yr, zsum, pbuf, prec, fin,
    gp, gp1, gpf, gcol_s, gcol_r,
    loc_sem, wsend, wrecv, wfs, wfr, hs, hr, xss, xrs, yss, yrs, zss, zrs,
):
    a = lax.axis_index("azi")
    rad = lax.axis_index("rad")
    x = lax.axis_index("batch")
    core = lax.rem(a, 2)
    zlo = lax.rem(a // 2, 4)
    y = a // 8

    def dev(azi, r, b):
        return {"azi": azi, "rad": r, "batch": b}

    def signal(target):
        pl.semaphore_signal(barrier, inc=1, device_id=target, device_id_type=pl.DeviceIdType.MESH)

    def remote(src, dst, ss, rs, target):
        return pltpu.make_async_remote_copy(
            src_ref=src, dst_ref=dst, send_sem=ss, recv_sem=rs,
            device_id=target, device_id_type=pl.DeviceIdType.MESH,
        )

    other = dev(a + 1 - 2 * core, rad, x)
    up = dev(lax.rem(a + 63, 64), rad, x)
    down = dev(lax.rem(a + 1, 64), rad, x)
    band = dev(a, 1 - rad, x)
    x_peers = [dev(a, rad, lax.rem(x + d, 4)) for d in (1, 2, 3)]
    y_peers = [dev(lax.rem(y + d, 8) * 8 + zlo * 2 + core, rad, x) for d in range(1, 8)]
    own_home = zlo == x

    barrier = pltpu.get_barrier_semaphore()
    for target in [other, up, down, band] + x_peers + y_peers:
        signal(target)
    for cs in range(2):
        for zh in range(2):
            for zl in range(4):
                is_self = own_home & (core == cs) & (rad == zh) & (zlo == zl)

                @pl.when(jnp.logical_not(is_self))
                def _():
                    signal(dev((y * 4 + zl) * 2 + cs, zh, zlo))

    def shard_rows(w):
        return w.at[:, pl.ds(pl.multiple_of(64 * x, 64), 64), :]

    def half_rows(w, xi, k):
        return w.at[:, pl.ds(pl.multiple_of(64 * xi + 32 * k, 32), 32), :]

    lsnap = pltpu.make_async_copy(snap_hbm, snap.at[1:17], loc_sem.at[0])
    lw1 = pltpu.make_async_copy(w1_hbm, shard_rows(w1), loc_sem.at[1])
    lw2 = pltpu.make_async_copy(w2_hbm, shard_rows(w2), loc_sem.at[2])
    lcot = pltpu.make_async_copy(cot_hbm, cotr.at[4:12], loc_sem.at[3])
    for c in (lw1, lsnap, lcot, lw2):
        c.start()
    pl.semaphore_wait(barrier, jnp.where(own_home, 29, 30))

    def gather_send(w, w_hbm, base):
        out = []
        for d in range(3):
            src = w_hbm.at[:, pl.ds(pl.multiple_of(32 * core, 32), 32), :]
            c = remote(src, half_rows(w, x, core), wsend.at[base + d], wrecv.at[base + d], x_peers[d])
            c.start()
            out.append(c)
        return out

    def gather_forward(w, sends, base):
        out = []
        for d in range(3):
            sends[d].wait_recv()
            xi = lax.rem(x + 3 - d, 4)
            part = half_rows(w, xi, core)
            c = remote(part, part, wfs.at[base + d], wfr.at[base + d], other)
            c.start()
            out.append(c)
        return out

    g1 = gather_send(w1, w1_hbm, 0)
    hsnap = remote(snap_hbm.at[15], snap.at[0], hs.at[0], hr.at[0], down)
    hsnap.start()
    hcot_d = remote(cot_hbm.at[4:8], cotr.at[0:4], hs.at[1], hr.at[1], down)
    hcot_d.start()
    hcot_u = remote(cot_hbm.at[0:4], cotr.at[12:16], hs.at[2], hr.at[2], up)
    hcot_u.start()

    row_i = lax.broadcasted_iota(jnp.int32, (192, 128), 0)
    col_i = lax.broadcasted_iota(jnp.int32, (192, 128), 1)
    pick = jnp.where(col_i == 2 * lax.rem(row_i, 64) + row_i // 64 - 1, 1.0, 0.0).astype(BF)

    def split_row(e):
        got = dot_nn(pick, snap[e])
        for n in range(3):
            xs[n, e % 2, e // 2] = got[64 * n : 64 * n + 64].astype(BF)
        colf[e : e + 1, :] = got[191:192]

    colf[...] = jnp.zeros_like(colf)
    lsnap.wait()
    for e in range(1, 17):
        split_row(e)
    hsnap.wait()
    split_row(0)
    cols_s[...] = colf[...].astype(BF)
    hcols = remote(cols_s, cols_r, hs.at[3], hr.at[3], band)
    hcols.start()

    def edges(field, out):
        for r in range(16):
            low = field[r, 0:16, :].astype(F32)[0:4]
            high = field[r, 48:64, :].astype(F32)[12:16]
            edgef[4 * r : 4 * r + 4, :] = jnp.where(rad == 0, high, low)
        out[...] = edgef[...].astype(BF)

    def shifted(field, edge, sh):
        got = edge[...].astype(F32)
        for r in range(16):
            extf[r, 8:72, :] = field[r].astype(F32)
            part = got[4 * r : 4 * r + 4]
            extf[r, 4:8, :] = jnp.where(rad == 1, part, 0.0)
            extf[r, 72:76, :] = jnp.where(rad == 0, part, 0.0)
            sh[1, r] = field[r]
            sh[2, r] = extf[r, 4:68, :].astype(BF)
            sh[0, r] = extf[r, 12:76, :].astype(BF)

    lcot.wait()
    hcot_d.wait()
    hcot_u.wait()
    edges(cotr, cedge_s)
    hcedge = remote(cedge_s, cedge_r, hs.at[4], hr.at[4], band)
    hcedge.start()

    hcols.wait()
    in_row = lax.broadcasted_iota(jnp.int32, (16, 256), 0)
    colv = jnp.where(rad == 1, cols_r[...].astype(F32), 0.0)
    for e in range(17):
        tile = xs[0, e % 2, e // 2, 0:16, :].astype(F32)
        xs[0, e % 2, e // 2, 0:16, :] = jnp.where(in_row == 0, colv[e : e + 1], tile).astype(BF)

    f1 = gather_forward(w1, g1, 0)
    lw1.wait()

    hcedge.wait()
    shifted(cotr, cedge_r, cot_sh)
    mine = pl.ds(pl.multiple_of(128 * core, 128), 128)
    theirs = pl.ds(pl.multiple_of(128 * (1 - core), 128), 128)
    lhalf = pltpu.make_async_copy(cot_sh.at[:, :, :, mine], cot_h.at[core], loc_sem.at[4])
    lhalf.start()
    hhalf = remote(cot_sh.at[:, :, :, theirs], cot_h.at[core], hs.at[5], hr.at[5], other)
    hhalf.start()

    for d in range(3):
        f1[d].wait()
    for d in range(3):
        g1[d].wait_send()
    g2 = gather_send(w2, w2_hbm, 3)

    def conv1(b, _):
        at_row = 4 * b
        total = jnp.zeros((256, 256), F32)
        for t in range(9):
            m, n = t // 3, t % 3
            win = xs[n, m % 2, pl.ds(at_row + m // 2, 4)].reshape(256, 256)
            total = total + dot_nt(win, w1[t])
        pre[pl.ds(pl.multiple_of(256 * b, 256), 256), :] = total
        sig = 1.0 / (1.0 + jnp.exp(-total))
        act = (total * sig).astype(BF)
        actr[pl.ds(4 + at_row, 4)] = act.reshape(4, 64, 256)
        act_pair[core, pl.ds(pl.multiple_of(256 * b, 256), 256), :] = act
        return 0

    lax.fori_loop(0, 2, conv1, 0)
    hact = remote(act_pair.at[core], act_pair.at[core], hs.at[6], hr.at[6], other)
    hact.start()
    hact_d = remote(actr.at[8:12], actr.at[0:4], hs.at[7], hr.at[7], down)
    hact_d.start()
    hact_u = remote(actr.at[4:8], actr.at[12:16], hs.at[8], hr.at[8], up)
    hact_u.start()
    lhalf.wait()
    hhalf.wait()
    hact.wait()
    for k in range(2):
        at[:, 512 * k : 512 * k + 512] = act_pair[k].T

    def window(k, t):
        m, n = t // 3, t % 3
        return cot_h[k, n, 8 - 4 * m : 16 - 4 * m].reshape(512, 128)

    def put(t, value):
        first = 256 * t
        for q in range(32):
            lo, hi = max(72 * q, first), min(72 * q + 72, first + 256)
            if lo < hi:
                gbuf[q % 4, q // 4, lo - 72 * q : hi - 72 * q, :] = value[lo - first : hi - first] * (1.0 / 512.0)

    for t in range(0, 8, 2):
        total = jnp.zeros((256, 256), F32)
        for k in range(2):
            both = jnp.concatenate([window(k, t), window(k, t + 1)], axis=1)
            total = total + dot_nn(at[:, 512 * k : 512 * k + 512], both)
        put(t, total[:, 0:128])
        put(t + 1, total[:, 128:256])
    total = jnp.zeros((256, 128), F32)
    for k in range(2):
        total = total + dot_nn(at[:, 512 * k : 512 * k + 512], window(k, 8))
    put(8, total)
    for i in range(4):
        for j in range(8):
            gbuf[i, j, 72:80, :] = jnp.zeros((8, 128), F32)
    for i in range(4):
        xbuf[i] = gbuf[i].astype(BF)
    xc = []
    for d in range(3):
        c = remote(xbuf.at[lax.rem(x + 1 + d, 4)], xr.at[d], xss.at[d], xrs.at[d], x_peers[d])
        c.start()
        xc.append(c)

    hact_d.wait()
    hact_u.wait()
    edges(actr, aedge_s)
    haedge = remote(aedge_s, aedge_r, hs.at[9], hr.at[9], band)
    haedge.start()
    f2 = gather_forward(w2, g2, 3)
    lw2.wait()
    haedge.wait()
    shifted(actr, aedge_r, act_sh)

    for d in range(3):
        xc[d].wait()
    for j in range(8):
        s = gbuf[x, j]
        for d in range(3):
            s = s + xr[d, j].astype(F32)
        ysum[j] = s
        ybuf[j] = s.astype(BF)
    yc = []
    for d in range(7):
        c = remote(ybuf.at[lax.rem(y + 1 + d, 8)], yr.at[d], yss.at[d], yrs.at[d], y_peers[d])
        c.start()
        yc.append(c)

    for d in range(3):
        f2[d].wait()
    for d in range(3):
        g2[d].wait_send()

    def back(b, _):
        at_row = 4 * b
        cells = pl.ds(pl.multiple_of(256 * b, 256), 256)
        total = cot_sh[1, pl.ds(4 + at_row, 4)].reshape(256, 256).astype(F32)
        for t in range(9):
            m, n = t // 3, t % 3
            win = cot_sh[n, pl.ds(at_row + 8 - 4 * m, 4)].reshape(256, 256)
            total = total + dot_nn(win, w2[t])
        v = pre[cells, :]
        s = 1.0 / (1.0 + jnp.exp(-v))
        g = (total * (s * (1.0 + v * (1.0 - s)))).astype(BF)
        gp[pl.ds(at_row, 4)] = g.reshape(4, 64, 256)
        return 0

    lax.fori_loop(0, 2, back, 0)
    hgp = remote(gp.at[0], gp.at[8], hs.at[10], hr.at[10], up)
    hgp.start()

    for d in range(7):
        yc[d].wait()
    s = ysum[y]
    for d in range(7):
        s = s + yr[d].astype(F32)
    zsum[...] = s
    for p in range(16):
        pbuf[p] = zsum[(9 * p) // 2 : (9 * p) // 2 + 8, :]
    slot = core * 8 + rad * 4 + zlo
    zc = []
    for p in range(16):
        c1, zh, xp = p // 8, (p // 4) % 2, p % 4
        is_self = own_home & (core == c1) & (rad == zh) & (x == xp)
        rc = remote(pbuf.at[p], prec.at[slot], zss.at[p], zrs.at[slot], dev((y * 4 + x) * 2 + c1, zh, xp))
        lc = pltpu.make_async_copy(pbuf.at[p], prec.at[slot], zrs.at[slot])

        @pl.when(is_self)
        def _():
            lc.start()

        @pl.when(jnp.logical_not(is_self))
        def _():
            rc.start()

        zc.append((is_self, rc))

    def ahead(b, _):
        at_row = 4 * b
        total = act_sh[1, pl.ds(4 + at_row, 4)].reshape(256, 256).astype(F32)
        for t in range(9):
            m, n = t // 3, t % 3
            win = act_sh[2 - n, pl.ds(at_row + 4 * m, 4)].reshape(256, 256)
            total = total + dot_nt(win, w2[t])
        enc_ref[pl.ds(at_row, 4)] = total.astype(BF).reshape(4, 64, 256)
        return 0

    hgp.wait()
    for r in range(9):
        gpf[r, 0:64, :] = gp[r].astype(F32)
        colf[r : r + 1, :] = gpf[r, 0:1, :]
    gcol_s[...] = colf[0:16, :].astype(BF)
    hgcol = remote(gcol_s, gcol_r, hs.at[11], hr.at[11], band)
    hgcol.start()
    lax.fori_loop(0, 2, ahead, 0)
    hgcol.wait()
    colv = jnp.where(rad == 0, gcol_r[...].astype(F32), 0.0)
    for r in range(9):
        gpf[r, 64:65, :] = colv[r : r + 1]
        gp1[r] = gpf[r, 1:65, :].astype(BF)

    row_q = lax.broadcasted_iota(jnp.int32, (128, 128), 0)
    col_q = lax.broadcasted_iota(jnp.int32, (128, 128), 1)
    weave = jnp.where(col_q == lax.rem(row_q, 2) * 64 + row_q // 2, 1.0, 0.0).astype(BF)
    ptaps = (((1, 0),), ((2, 0), (0, 1)))

    def inward(b, _):
        at_row = 4 * b
        for rp in range(2):
            halves = []
            for cp in range(2):
                total = jnp.zeros((256, 256), F32)
                for m, rs in ptaps[rp]:
                    for n, cs in ptaps[cp]:
                        field = gp1 if cs else gp
                        win = field[pl.ds(at_row + rs, 4)].reshape(256, 256)
                        total = total + dot_nn(win, w1[3 * m + n])
                halves.append(total.astype(BF).reshape(4, 64, 256))
            for i in range(4):
                pair = jnp.concatenate([halves[0][i], halves[1][i]], axis=0)
                ing_ref[2 * (at_row + i) + rp] = dot_nn(weave, pair).astype(BF)
        return 0

    lax.fori_loop(0, 2, inward, 0)

    for s in range(16):
        pltpu.make_async_copy(pbuf.at[0], prec.at[s], zrs.at[s]).wait()
    for k in range(2):
        s = prec[8 * k]
        for i in range(1, 8):
            s = s + prec[8 * k + i]
        for i in range(5):
            fin[2 * i + k : 2 * i + k + 1, :] = s[i : i + 1]
    kg_ref[...] = jnp.where(lax.rem(x, 2) == 0, fin[0:9, :], fin[1:10, :])
    for is_self, rc in zc:
        @pl.when(jnp.logical_not(is_self))
        def _():
            rc.wait_send()


def body(snapshots, first_kernel, second_kernel, cotangent):
    def vm(shape, kind=BF):
        return pltpu.VMEM(shape, kind)

    dma = pltpu.SemaphoreType.DMA
    scratch = [
        vm((17, 128, 256)), vm((3, 2, 9, 64, 256)), vm((32, 256), F32), vm((32, 256)), vm((32, 256)),
        vm((9, 256, 256)), vm((9, 256, 256)), vm((16, 64, 256)), vm((3, 16, 64, 256)),
        vm((64, 256), F32), vm((64, 256)), vm((64, 256)), vm((64, 256)), vm((64, 256)),
        vm((16, 80, 256), F32), vm((2, 3, 16, 64, 128)), vm((16, 64, 256)), vm((2, 512, 256)),
        vm((3, 16, 64, 256)), vm((512, 256), F32), vm((256, 1024)),
        vm((4, 8, 80, 128), F32), vm((4, 8, 80, 128)), vm((3, 8, 80, 128)),
        vm((8, 80, 128), F32), vm((8, 80, 128)), vm((7, 80, 128)),
        vm((80, 128), F32), vm((16, 8, 128), F32), vm((16, 8, 128), F32), vm((16, 128), F32),
        vm((9, 64, 256)), vm((9, 64, 256)), vm((9, 80, 256), F32), vm((16, 256)), vm((16, 256)),
        dma((5,)), dma((6,)), dma((6,)), dma((6,)), dma((6,)), dma((12,)), dma((12,)),
        dma((3,)), dma((3,)), dma((7,)), dma((7,)), dma((16,)), dma((16,)),
    ]
    enc, ing, kg = pl.pallas_call(
        kernel,
        name="section",
        out_shape=(
            jax.ShapeDtypeStruct((8, 64, 256), BF),
            jax.ShapeDtypeStruct((16, 128, 256), BF),
            jax.ShapeDtypeStruct((9, 128), F32),
        ),
        in_specs=[pl.BlockSpec(memory_space=pl.ANY)] * 4,
        out_specs=[pl.BlockSpec(memory_space=pltpu.VMEM)] * 3,
        scratch_shapes=scratch,
        compiler_params=pltpu.CompilerParams(
            collective_id=0, has_side_effects=True, vmem_limit_bytes=56 << 20
        ),
    )(
        snapshots[0],
        jnp.swapaxes(first_kernel, 1, 2),
        jnp.swapaxes(second_kernel, 1, 2),
        cotangent[0],
    )
    return enc[None], ing[None], kg.reshape(1152)


def solution(mesh):
    return jax.shard_map(
        body,
        mesh=mesh,
        in_specs=(
            P("batch", "azi", "rad", None),
            P(None, None, "batch"),
            P(None, None, "batch"),
            P("batch", "azi", "rad", None),
        ),
        out_specs=(
            P("batch", "azi", "rad", None),
            P("batch", "azi", "rad", None),
            P(("azi", "rad", "batch")),
        ),
        check_vma=False,
    )
```

```python
import jax
import jax.numpy as jnp
from jax import lax
from jax.experimental import pallas as pl
from jax.experimental.pallas import tpu as pltpu
from jax.sharding import PartitionSpec as P

BF = jnp.bfloat16
F32 = jnp.float32
SHIFTS = (4, 0, -4)


def dot_nt(a, b):
    return lax.dot_general(a, b, (((1,), (1,)), ((), ())), preferred_element_type=F32)


def dot_nn(a, b):
    return lax.dot_general(a, b, (((1,), (0,)), ((), ())), preferred_element_type=F32)


def kernel(
    snap_hbm, w1_hbm, w2_hbm, cot_hbm,
    enc_ref, ing_ref, kg_ref,
    snap, xs, colf, cols_s, cols_r, cols_c, w1, w2, cot24, cot_sh, cot_h, edgef, cedge_s, cedge_r, aedge_s, aedge_r,
    extf, actr, act_pair, act_sh, pre, at, g1, g2, xbuf1, xr1, s1, ybuf1, yr1, ybuf2, yr2, s2, xbuf2, xr2,
    zsum, pbuf, prec, fin, gp, gp1, gpf, gcol_s, gcol_r,
    loc_sem, wsend, wrecv, wfs, wfr, hs, hr, xss, xrs, yss, yrs, zss, zrs,
):
    a = lax.axis_index("azi")
    rad = lax.axis_index("rad")
    x = lax.axis_index("batch")
    core = lax.rem(a, 2)
    zlo = lax.rem(a // 2, 4)
    y = a // 8

    def dev(azi, r, b):
        return {"azi": azi, "rad": r, "batch": b}

    def signal(target):
        pl.semaphore_signal(barrier, inc=1, device_id=target, device_id_type=pl.DeviceIdType.MESH)

    def remote(src, dst, ss, rs, target):
        return pltpu.make_async_remote_copy(
            src_ref=src, dst_ref=dst, send_sem=ss, recv_sem=rs,
            device_id=target, device_id_type=pl.DeviceIdType.MESH,
        )

    other = dev(a + 1 - 2 * core, rad, x)
    up = dev(lax.rem(a + 63, 64), rad, x)
    down = dev(lax.rem(a + 1, 64), rad, x)
    band = dev(a, 1 - rad, x)
    step = 2 * core - 1
    near = dev(lax.rem(a + 64 + step, 64), rad, x)
    far = dev(lax.rem(a + 64 + 2 * step, 64), rad, x)
    far_from = dev(lax.rem(a + 64 - 2 * step, 64), rad, x)

    def across(target):
        return dev(target["azi"], 1 - rad, x)

    x_peers = [dev(a, rad, lax.rem(x + d, 4)) for d in (1, 2, 3)]
    y_peers = [dev(lax.rem(y + d, 8) * 8 + zlo * 2 + core, rad, x) for d in range(1, 8)]
    own_home = zlo == x

    barrier = pltpu.get_barrier_semaphore()
    for target in [other, up, down, band, far_from, across(other), across(near), across(far_from), across(up)] + x_peers + y_peers:
        signal(target)
    for cs in range(2):
        for zh in range(2):
            for zl in range(4):
                is_self = own_home & (core == cs) & (rad == zh) & (zlo == zl)

                @pl.when(jnp.logical_not(is_self))
                def _():
                    signal(dev((y * 4 + zl) * 2 + cs, zh, zlo))

    def shard_rows(w):
        return w.at[:, pl.ds(pl.multiple_of(64 * x, 64), 64), :]

    def half_rows(w, xi, k):
        return w.at[:, pl.ds(pl.multiple_of(64 * xi + 32 * k, 32), 32), :]

    lsnap = pltpu.make_async_copy(snap_hbm, snap.at[1:17], loc_sem.at[0])
    lw1 = pltpu.make_async_copy(w1_hbm, shard_rows(w1), loc_sem.at[1])
    lw2 = pltpu.make_async_copy(w2_hbm, shard_rows(w2), loc_sem.at[2])
    own_rows = pl.ds(4 + 8 * core, 8)
    lcot = pltpu.make_async_copy(cot_hbm, cot24.at[own_rows], loc_sem.at[3])
    for c in (lcot, lsnap, lw1, lw2):
        c.start()

    def edge(tile_of, out, r):
        low = tile_of(0).astype(F32)[0:4]
        high = tile_of(48).astype(F32)[12:16]
        out[4 * r : 4 * r + 4, :] = jnp.where(rad == 0, high, low)

    lcot.wait()
    for r in range(8):
        edge(lambda c: cot24[4 + 8 * core + r, c : c + 16, :], edgef, r)
    cedge_s[...] = edgef[0:32, :].astype(BF)
    pl.semaphore_wait(barrier, jnp.where(own_home, 34, 35))

    def gather_send(w, w_hbm, base):
        out = []
        for d in (1, 0, 2):
            src = w_hbm.at[:, pl.ds(pl.multiple_of(32 * core, 32), 32), :]
            c = remote(src, half_rows(w, x, core), wsend.at[base + d], wrecv.at[base + d], x_peers[d])
            c.start()
            out.append(c)
        return [out[1], out[0], out[2]]

    def gather_forward(w, sends, base):
        out = []
        for d in (0, 2, 1):
            sends[d].wait_recv()
            xi = lax.rem(x + 3 - d, 4)
            part = half_rows(w, xi, core)
            c = remote(part, part, wfs.at[base + d], wfr.at[base + d], other)
            c.start()
            out.append(c)
        return out

    g1s = gather_send(w1, w1_hbm, 0)
    hsnap = remote(snap_hbm.at[15], snap.at[0], hs.at[0], hr.at[0], down)
    hsnap.start()
    edge_rows = pl.ds(4 * core, 4)
    far_rows = pl.ds(20 * (1 - core), 4)
    half = pl.ds(pl.multiple_of(128 * core, 128), 128)
    cot_halo = [
        remote(cot_hbm.at[edge_rows], cot24.at[far_rows], hs.at[1], hr.at[1], near),
        remote(cot_hbm.at[edge_rows, :, half], cot24.at[far_rows, :, half], hs.at[2], hr.at[2], far),
        remote(cot_hbm, cot24.at[own_rows], hs.at[4], hr.at[4], other),
    ]
    mid = pl.ds(pl.multiple_of(16 + 32 * core, 16), 32)
    tip = pl.ds(pl.multiple_of(80 * (1 - core), 16), 16)
    tip_s = pl.ds(pl.multiple_of(16 * core, 16), 16)
    for i, target in ((12, band), (13, across(other))):
        cot_halo.append(remote(cedge_s, cedge_r.at[mid], hs.at[i], hr.at[i], target))
    for i, target in ((14, across(near)), (15, across(far))):
        cot_halo.append(remote(cedge_s.at[tip_s], cedge_r.at[tip], hs.at[i], hr.at[i], target))
    for c in cot_halo:
        c.start()

    row_i = lax.broadcasted_iota(jnp.int32, (192, 128), 0)
    col_i = lax.broadcasted_iota(jnp.int32, (192, 128), 1)
    pick = jnp.where(col_i == 2 * lax.rem(row_i, 64) + row_i // 64 - 1, 1.0, 0.0).astype(BF)

    def split_row(e):
        got = dot_nn(pick, snap[e])
        for n in range(3):
            xs[n, e % 2, e // 2] = got[64 * n : 64 * n + 64].astype(BF)
        colf[e : e + 1, :] = got[191:192]

    lsnap.wait()
    for e in range(1, 17):
        split_row(e)
    cols_s[...] = colf[1:17, :].astype(BF)
    hcols = remote(cols_s, cols_r, hs.at[3], hr.at[3], band)
    hcols.start()
    hcorner = remote(cols_s, cols_c, hs.at[5], hr.at[5], across(down))
    hcorner.start()

    for c in cot_halo:
        c.wait()
    got = cedge_r[...].astype(F32)
    for r in range(24):
        extf[r, 8:72, :] = cot24[r].astype(F32)
        part = got[4 * r : 4 * r + 4]
        extf[r, 4:8, :] = jnp.where(rad == 1, part, 0.0)
        extf[r, 72:76, :] = jnp.where(rad == 0, part, 0.0)
        for n, start in ((0, 12), (1, 8), (2, 4)):
            value = extf[r, start : start + 64, :].astype(BF)
            cot_sh[n, r] = value
            cot_h[n, r] = jnp.where(core == 0, value[:, 0:128], value[:, 128:256])

    f1 = gather_forward(w1, g1s, 0)
    g2s = gather_send(w2, w2_hbm, 3)

    hsnap.wait()
    split_row(0)
    hcols.wait()
    hcorner.wait()
    in_row = lax.broadcasted_iota(jnp.int32, (16, 256), 0)
    colv = jnp.where(rad == 1, cols_r[...].astype(F32), 0.0)
    corner = jnp.where(rad == 1, cols_c[...].astype(F32), 0.0)
    for e in range(17):
        tile = xs[0, e % 2, e // 2, 0:16, :].astype(F32)
        side = colv[e - 1 : e] if e else corner[15:16]
        xs[0, e % 2, e // 2, 0:16, :] = jnp.where(in_row == 0, side, tile).astype(BF)
    lw1.wait()
    for d in range(3):
        f1[d].wait()
        g1s[d].wait_send()

    def edges(field, out):
        for r in range(16):
            edge(lambda c: field[r, c : c + 16, :], edgef, r)
        out[...] = edgef[...].astype(BF)

    def shifted(field, edge_got, sh):
        got = edge_got[...].astype(F32)
        for r in range(16):
            extf[r, 8:72, :] = field[r].astype(F32)
            part = got[4 * r : 4 * r + 4]
            extf[r, 4:8, :] = jnp.where(rad == 1, part, 0.0)
            extf[r, 72:76, :] = jnp.where(rad == 0, part, 0.0)
            sh[1, r] = field[r]
            sh[2, r] = extf[r, 4:68, :].astype(BF)
            sh[0, r] = extf[r, 12:76, :].astype(BF)

    def conv1(b, _):
        at_row = 4 * b
        total = jnp.zeros((256, 256), F32)
        for t in range(9):
            m, n = t // 3, t % 3
            win = xs[n, m % 2, pl.ds(at_row + m // 2, 4)].reshape(256, 256)
            total = total + dot_nt(win, w1[t])
        pre[pl.ds(pl.multiple_of(256 * b, 256), 256), :] = total
        sig = 1.0 / (1.0 + jnp.exp(-total))
        act = (total * sig).astype(BF)
        actr[pl.ds(4 + at_row, 4)] = act.reshape(4, 64, 256)
        act_pair[core, pl.ds(pl.multiple_of(256 * b, 256), 256), :] = act
        return 0

    lax.fori_loop(0, 2, conv1, 0)
    hact = remote(act_pair.at[core], act_pair.at[core], hs.at[6], hr.at[6], other)
    hact.start()
    hact_d = remote(actr.at[8:12], actr.at[0:4], hs.at[7], hr.at[7], down)
    hact_d.start()
    hact_u = remote(actr.at[4:8], actr.at[12:16], hs.at[8], hr.at[8], up)
    hact_u.start()
    hact.wait()
    for k in range(2):
        at[:, 512 * k : 512 * k + 512] = act_pair[k].T

    def window(t):
        m, n = t // 3, t % 3
        return cot_h[n, 8 - 4 * m : 24 - 4 * m].reshape(1024, 128)

    def put(t, value):
        first = 256 * t
        value = value * (1.0 / 512.0)
        for q in range(32):
            for lo, hi in ((72 * q, 72 * q + 56), (72 * q + 56, 72 * q + 72)):
                part = hi - lo
                a0, a1 = max(lo, first), min(hi, first + 256)
                if a0 >= a1:
                    continue
                rows = value[a0 - first : a1 - first]
                if part == 56:
                    g1[q % 4, 56 * (q // 4) + a0 - lo : 56 * (q // 4) + a1 - lo, :] = rows
                else:
                    g2[q // 4, 16 * (q % 4) + a0 - lo : 16 * (q % 4) + a1 - lo, :] = rows

    for t in range(0, 8, 2):
        both = jnp.concatenate([window(t), window(t + 1)], axis=1)
        total = dot_nn(at[...], both)
        put(t, total[:, 0:128])
        put(t + 1, total[:, 128:256])
    put(8, dot_nn(at[...], window(8)))
    for i in range(4):
        xbuf1[i] = g1[i].astype(BF)
    xc1 = []
    for d in (1, 0, 2):
        c = remote(xbuf1.at[lax.rem(x + 1 + d, 4)], xr1.at[d], xss.at[d], xrs.at[d], x_peers[d])
        c.start()
        xc1.append(c)
    for i in range(8):
        ybuf2[i] = g2[i].astype(BF)
    yc2 = []
    for d in (3, 2, 4, 1, 5, 0, 6):
        c = remote(ybuf2.at[lax.rem(y + 1 + d, 8)], yr2.at[d], yss.at[d], yrs.at[d], y_peers[d])
        c.start()
        yc2.append(c)

    hact_d.wait()
    hact_u.wait()
    edges(actr, aedge_s)
    haedge = remote(aedge_s, aedge_r, hs.at[9], hr.at[9], band)
    haedge.start()
    f2 = gather_forward(w2, g2s, 3)
    lw2.wait()

    for c in xc1:
        c.wait()
    for j in range(8):
        rows = slice(56 * j, 56 * j + 56)
        s = g1[x, rows, :]
        for d in range(3):
            s = s + xr1[d, rows, :].astype(F32)
        s1[j, 0:56, :] = s
        s1[j, 56:64, :] = jnp.zeros((8, 128), F32)
        ybuf1[j] = s1[j].astype(BF)
    yc1 = []
    for d in (3, 2, 4, 1, 5, 0, 6):
        c = remote(ybuf1.at[lax.rem(y + 1 + d, 8)], yr1.at[d], yss.at[7 + d], yrs.at[7 + d], y_peers[d])
        c.start()
        yc1.append(c)
    for c in yc2:
        c.wait()
    s = g2[y]
    for d in range(7):
        s = s + yr2[d].astype(F32)
    for i in range(4):
        s2[i] = s[16 * i : 16 * i + 16]
    for i in range(4):
        xbuf2[i] = s2[i].astype(BF)
    xc2 = []
    for d in (1, 0, 2):
        c = remote(xbuf2.at[lax.rem(x + 1 + d, 4)], xr2.at[d], xss.at[3 + d], xrs.at[3 + d], x_peers[d])
        c.start()
        xc2.append(c)

    for d in range(3):
        f2[d].wait()
        g2s[d].wait_send()

    def back(b, _):
        at_row = 4 * b
        cells = pl.ds(pl.multiple_of(256 * b, 256), 256)
        total = cot24[pl.ds(4 + 8 * core + at_row, 4)].reshape(256, 256).astype(F32)
        for t in range(9):
            m, n = t // 3, t % 3
            win = cot_sh[n, pl.ds(8 * core + at_row + 8 - 4 * m, 4)].reshape(256, 256)
            total = total + dot_nn(win, w2[t])
        v = pre[cells, :]
        s = 1.0 / (1.0 + jnp.exp(-v))
        g = (total * (s * (1.0 + v * (1.0 - s)))).astype(BF)
        gp[pl.ds(at_row, 4)] = g.reshape(4, 64, 256)
        return 0

    lax.fori_loop(0, 2, back, 0)
    hgp = remote(gp.at[0], gp.at[8], hs.at[10], hr.at[10], up)
    hgp.start()
    haedge.wait()
    shifted(actr, aedge_r, act_sh)

    for c in xc2:
        c.wait()
    s = s2[x]
    for d in range(3):
        s = s + xr2[d].astype(F32)
    zsum[56:72, :] = s
    for c in yc1:
        c.wait()
    s = s1[y, 0:56, :]
    for d in range(7):
        s = s + yr1[d].astype(F32)[0:56]
    zsum[0:56, :] = s
    zsum[72:80, :] = jnp.zeros((8, 128), F32)
    for p in range(16):
        pbuf[p] = zsum[(9 * p) // 2 : (9 * p) // 2 + 8, :]
    slot = core * 8 + rad * 4 + zlo
    zc = []
    for p in range(16):
        c1, zh, xp = p // 8, (p // 4) % 2, p % 4
        is_self = own_home & (core == c1) & (rad == zh) & (x == xp)
        rc = remote(pbuf.at[p], prec.at[slot], zss.at[p], zrs.at[slot], dev((y * 4 + x) * 2 + c1, zh, xp))
        lc = pltpu.make_async_copy(pbuf.at[p], prec.at[slot], zrs.at[slot])

        @pl.when(is_self)
        def _():
            lc.start()

        @pl.when(jnp.logical_not(is_self))
        def _():
            rc.start()

        zc.append((is_self, rc))

    def ahead(b, _):
        at_row = 4 * b
        total = act_sh[1, pl.ds(4 + at_row, 4)].reshape(256, 256).astype(F32)
        for t in range(9):
            m, n = t // 3, t % 3
            win = act_sh[2 - n, pl.ds(at_row + 4 * m, 4)].reshape(256, 256)
            total = total + dot_nt(win, w2[t])
        enc_ref[pl.ds(at_row, 4)] = total.astype(BF).reshape(4, 64, 256)
        return 0

    hgp.wait()
    for r in range(9):
        gpf[r, 0:64, :] = gp[r].astype(F32)
        colf[r : r + 1, :] = gpf[r, 0:1, :]
    gcol_s[...] = colf[0:16, :].astype(BF)
    hgcol = remote(gcol_s, gcol_r, hs.at[11], hr.at[11], band)
    hgcol.start()
    lax.fori_loop(0, 2, ahead, 0)
    hgcol.wait()
    colv = jnp.where(rad == 0, gcol_r[...].astype(F32), 0.0)
    for r in range(9):
        gpf[r, 64:65, :] = colv[r : r + 1]
        gp1[r] = gpf[r, 1:65, :].astype(BF)

    row_q = lax.broadcasted_iota(jnp.int32, (128, 128), 0)
    col_q = lax.broadcasted_iota(jnp.int32, (128, 128), 1)
    weave = jnp.where(col_q == lax.rem(row_q, 2) * 64 + row_q // 2, 1.0, 0.0).astype(BF)
    ptaps = (((1, 0),), ((2, 0), (0, 1)))

    def inward(b, _):
        at_row = 4 * b
        for rp in range(2):
            halves = []
            for cp in range(2):
                total = jnp.zeros((256, 256), F32)
                for m, rs in ptaps[rp]:
                    for n, cs in ptaps[cp]:
                        field = gp1 if cs else gp
                        win = field[pl.ds(at_row + rs, 4)].reshape(256, 256)
                        total = total + dot_nn(win, w1[3 * m + n])
                halves.append(total.astype(BF).reshape(4, 64, 256))
            for i in range(4):
                pair = jnp.concatenate([halves[0][i], halves[1][i]], axis=0)
                ing_ref[2 * (at_row + i) + rp] = dot_nn(weave, pair).astype(BF)
        return 0

    lax.fori_loop(0, 2, inward, 0)

    for s in range(16):
        pltpu.make_async_copy(pbuf.at[0], prec.at[s], zrs.at[s]).wait()
    for k in range(2):
        s = prec[8 * k]
        for i in range(1, 8):
            s = s + prec[8 * k + i]
        for i in range(5):
            fin[2 * i + k : 2 * i + k + 1, :] = s[i : i + 1]
    kg_ref[...] = jnp.where(lax.rem(x, 2) == 0, fin[0:9, :], fin[1:10, :])
    for is_self, rc in zc:
        @pl.when(jnp.logical_not(is_self))
        def _():
            rc.wait_send()


def body(snapshots, first_kernel, second_kernel, cotangent):
    def vm(shape, kind=BF):
        return pltpu.VMEM(shape, kind)

    dma = pltpu.SemaphoreType.DMA
    scratch = [
        vm((17, 128, 256)), vm((3, 2, 9, 64, 256)), vm((32, 256), F32), vm((16, 256)), vm((16, 256)), vm((16, 256)),
        vm((9, 256, 256)), vm((9, 256, 256)), vm((24, 64, 256)), vm((3, 24, 64, 256)), vm((3, 24, 64, 128)),
        vm((64, 256), F32), vm((32, 256)), vm((96, 256)), vm((64, 256)), vm((64, 256)),
        vm((24, 80, 256), F32), vm((16, 64, 256)), vm((2, 512, 256)),
        vm((3, 16, 64, 256)), vm((512, 256), F32), vm((256, 1024)),
        vm((4, 448, 128), F32), vm((8, 64, 128), F32), vm((4, 448, 128)), vm((3, 448, 128)),
        vm((8, 64, 128), F32), vm((8, 64, 128)), vm((7, 64, 128)), vm((8, 64, 128)), vm((7, 64, 128)),
        vm((4, 16, 128), F32), vm((4, 16, 128)), vm((3, 16, 128)),
        vm((80, 128), F32), vm((16, 8, 128), F32), vm((16, 8, 128), F32), vm((16, 128), F32),
        vm((9, 64, 256)), vm((9, 64, 256)), vm((9, 80, 256), F32), vm((16, 256)), vm((16, 256)),
        dma((4,)), dma((6,)), dma((6,)), dma((6,)), dma((6,)), dma((16,)), dma((16,)),
        dma((6,)), dma((6,)), dma((14,)), dma((14,)), dma((16,)), dma((16,)),
    ]
    enc, ing, kg = pl.pallas_call(
        kernel,
        name="section",
        out_shape=(
            pltpu.VMEM((8, 64, 256), BF),
            pltpu.VMEM((16, 128, 256), BF),
            pltpu.VMEM((9, 128), F32),
        ),
        in_specs=[pl.BlockSpec(memory_space=pl.ANY)] * 4,
        out_specs=[pl.BlockSpec(memory_space=pltpu.VMEM)] * 3,
        scratch_shapes=scratch,
        compiler_params=pltpu.CompilerParams(
            collective_id=0, has_side_effects=True, vmem_limit_bytes=56 << 20
        ),
    )(
        snapshots[0],
        jnp.swapaxes(first_kernel, 1, 2),
        jnp.swapaxes(second_kernel, 1, 2),
        cotangent[0],
    )
    return enc[None], ing[None], kg.reshape(1152)


def solution(mesh):
    return jax.shard_map(
        body,
        mesh=mesh,
        in_specs=(
            P("batch", "azi", "rad", None),
            P(None, None, "batch"),
            P(None, None, "batch"),
            P("batch", "azi", "rad", None),
        ),
        out_specs=(
            P("batch", "azi", "rad", None),
            P("batch", "azi", "rad", None),
            P(("azi", "rad", "batch")),
        ),
        check_vma=False,
    )
```

```python
import jax
import jax.numpy as jnp
from jax import lax
from jax.experimental import pallas as pl
from jax.experimental.pallas import tpu as pltpu
from jax.sharding import PartitionSpec as P

BF = jnp.bfloat16
F32 = jnp.float32
SHIFTS = (4, 0, -4)


def dot_nt(a, b):
    return lax.dot_general(a, b, (((1,), (1,)), ((), ())), preferred_element_type=F32)


def dot_nn(a, b):
    return lax.dot_general(a, b, (((1,), (0,)), ((), ())), preferred_element_type=F32)


def kernel(
    snap_hbm, w1_hbm, w2_hbm, cot_hbm,
    enc_ref, ing_ref, kg_ref,
    snap, xs, colf, cols_s, cols_r, cols_c, w1, w2, cot24, cot_sh, edgef, cedge_s, cedge_r, aedge_s, aedge_r,
    extf, actr, act_sh, pre, at, gt, g1, g2, xbuf1, xr1, s1, ybuf1, yr1, ybuf2, yr2, s2, xbuf2, xr2,
    zcom, zsum, pbuf, prec, fin, gp, gp1, gpf, gcol_s, gcol_r, gcol_c,
    loc_sem, wsend, wrecv, wfs, wfr, wzs, wzr, hs, hr, xss, xrs, yss, yrs, zss, zrs,
):
    a = lax.axis_index("azi")
    rad = lax.axis_index("rad")
    x = lax.axis_index("batch")
    core = lax.rem(a, 2)
    zlo = lax.rem(a // 2, 4)
    y = a // 8

    def dev(azi, r, b):
        return {"azi": azi, "rad": r, "batch": b}

    def signal(target):
        pl.semaphore_signal(barrier, inc=1, device_id=target, device_id_type=pl.DeviceIdType.MESH)

    def remote(src, dst, ss, rs, target):
        return pltpu.make_async_remote_copy(
            src_ref=src, dst_ref=dst, send_sem=ss, recv_sem=rs,
            device_id=target, device_id_type=pl.DeviceIdType.MESH,
        )

    other = dev(a + 1 - 2 * core, rad, x)
    up = dev(lax.rem(a + 63, 64), rad, x)
    down = dev(lax.rem(a + 1, 64), rad, x)
    band = dev(a, 1 - rad, x)
    step = 2 * core - 1
    near = dev(lax.rem(a + 64 + step, 64), rad, x)
    far = dev(lax.rem(a + 64 + 2 * step, 64), rad, x)
    far_from = dev(lax.rem(a + 64 - 2 * step, 64), rad, x)

    zi = 4 * rad + zlo

    def along_z(by):
        z2 = lax.rem(zi + 8 + by, 8)
        return dev(y * 8 + lax.rem(z2, 4) * 2 + core, z2 // 4, x)

    z_next, z_prev = along_z(1), along_z(-1)

    def across(target):
        return dev(target["azi"], 1 - rad, x)

    x_peers = [dev(a, rad, lax.rem(x + d, 4)) for d in (1, 2, 3)]
    y_peers = [dev(lax.rem(y + d, 8) * 8 + zlo * 2 + core, rad, x) for d in range(1, 8)]
    own_home = zlo == x

    barrier = pltpu.get_barrier_semaphore()
    for target in [other, up, down, band, far_from, across(other), across(near), across(far_from), across(up), across(down), z_next, z_prev] + x_peers + y_peers:
        signal(target)
    for cs in range(2):
        for zh in range(2):
            for zl in range(4):
                is_self = own_home & (core == cs) & (rad == zh) & (zlo == zl)

                @pl.when(jnp.logical_not(is_self))
                def _():
                    signal(dev((y * 4 + zl) * 2 + cs, zh, zlo))

    def shard_rows(w):
        return w.at[:, pl.ds(pl.multiple_of(64 * x, 64), 64), :]

    def half_rows(w, xi, k):
        return w.at[:, pl.ds(pl.multiple_of(64 * xi + 32 * k, 32), 32), :]

    own_snap = pl.ds(1 + 16 * core, 16)
    lsnap = pltpu.make_async_copy(snap_hbm, snap.at[own_snap], loc_sem.at[0])
    lw1 = pltpu.make_async_copy(w1_hbm, shard_rows(w1), loc_sem.at[1])
    lw2 = pltpu.make_async_copy(w2_hbm, shard_rows(w2), loc_sem.at[2])
    own_rows = pl.ds(4 + 8 * core, 8)
    lcot = pltpu.make_async_copy(cot_hbm, cot24.at[own_rows], loc_sem.at[3])
    for c in (lcot, lsnap, lw1, lw2):
        c.start()

    def edge(tile_of, out, r):
        low = tile_of(0).astype(F32)[0:4]
        high = tile_of(48).astype(F32)[12:16]
        out[4 * r : 4 * r + 4, :] = jnp.where(rad == 0, high, low)

    lcot.wait()
    for r in range(8):
        edge(lambda c: cot24[4 + 8 * core + r, c : c + 16, :], edgef, r)
    cedge_s[...] = edgef[0:32, :].astype(BF)
    pl.semaphore_wait(barrier, jnp.where(own_home, 37, 38))

    base = pl.ds(pl.multiple_of(32 * core, 32), 32)

    def part_of(w, xi, taps, k):
        return w.at[taps, pl.ds(pl.multiple_of(64 * xi + 32 * k, 32), 32), :]

    def gather_send(w, w_hbm, taps, at_sem):
        out = {}
        for d in (0, 2, 1):
            out[d] = remote(
                w_hbm.at[taps, base, :], part_of(w, x, taps, core), wsend.at[at_sem + d], wrecv.at[at_sem + d], x_peers[d]
            )
            out[d].start()
        return out

    def hand_on(w, d, taps, at_sem):
        part = part_of(w, lax.rem(x + 3 - d, 4), taps, core)
        c = remote(part, part, wfs.at[at_sem + d], wfr.at[at_sem + d], other)
        c.start()
        return c

    every = pl.ds(0, 9)
    g1s = gather_send(w1, w1_hbm, every, 0)
    hsnap = remote(snap_hbm, snap.at[own_snap], hs.at[0], hr.at[0], other)
    hsnap.start()
    row_near = remote(snap_hbm.at[15], snap.at[0], hs.at[6], hr.at[6], near)
    row_far = remote(snap_hbm.at[15], snap.at[0], hs.at[7], hr.at[6], far)

    @pl.when(core == 1)
    def _():
        row_near.start()
        row_far.start()

    edge_rows = pl.ds(4 * core, 4)
    far_rows = pl.ds(20 * (1 - core), 4)
    cot_halo = [
        remote(cot_hbm.at[edge_rows], cot24.at[far_rows], hs.at[1], hr.at[1], near),
        remote(cot_hbm.at[edge_rows], cot24.at[far_rows], hs.at[2], hr.at[2], far),
        remote(cot_hbm, cot24.at[own_rows], hs.at[4], hr.at[4], other),
    ]
    mid = pl.ds(pl.multiple_of(16 + 32 * core, 16), 32)
    tip = pl.ds(pl.multiple_of(80 * (1 - core), 16), 16)
    tip_s = pl.ds(pl.multiple_of(16 * core, 16), 16)
    for i, target in ((12, band), (13, across(other))):
        cot_halo.append(remote(cedge_s, cedge_r.at[mid], hs.at[i], hr.at[i], target))
    for i, target in ((14, across(near)), (15, across(far))):
        cot_halo.append(remote(cedge_s.at[tip_s], cedge_r.at[tip], hs.at[i], hr.at[i], target))
    for c in cot_halo:
        c.start()

    row_i = lax.broadcasted_iota(jnp.int32, (192, 128), 0)
    col_i = lax.broadcasted_iota(jnp.int32, (192, 128), 1)
    pick = jnp.where(col_i == 2 * lax.rem(row_i, 64) + row_i // 64 - 1, 1.0, 0.0).astype(BF)

    lsnap.wait()
    for r in range(16):
        e = 16 * core + 1 + r
        got = dot_nn(pick, snap[e])
        for n in range(3):
            xs[n, (1 + r) % 2, 8 * core + (1 + r) // 2] = got[64 * n : 64 * n + 64].astype(BF)
        colf[r : r + 1, :] = got[191:192]
    cols_s[...] = colf[0:16, :].astype(BF)
    col_rows = pl.ds(pl.multiple_of(16 * core, 16), 16)
    hcols = [
        remote(cols_s, cols_r.at[col_rows], hs.at[3], hr.at[3], band),
        remote(cols_s, cols_r.at[col_rows], hs.at[5], hr.at[5], across(other)),
    ]
    for c in hcols:
        c.start()
    tip_near = remote(cols_s, cols_c, hs.at[8], hr.at[8], across(near))
    tip_far = remote(cols_s, cols_c, hs.at[18], hr.at[8], across(far))

    @pl.when(core == 1)
    def _():
        tip_near.start()
        tip_far.start()

    for c in cot_halo:
        c.wait()
    got = cedge_r[...].astype(F32)
    for r in range(24):
        extf[r, 8:72, :] = cot24[r].astype(F32)
        part = got[4 * r : 4 * r + 4]
        extf[r, 4:8, :] = jnp.where(rad == 1, part, 0.0)
        extf[r, 72:76, :] = jnp.where(rad == 0, part, 0.0)
        for n, start in ((0, 12), (1, 8), (2, 4)):
            cot_sh[n, r] = extf[r, start : start + 64, :].astype(BF)

    hsnap.wait()
    for r in range(16):
        e = 16 * (1 - core) + 1 + r
        got = dot_nn(pick, snap[e])
        for n in range(3):
            xs[n, (1 + r) % 2, 8 * (1 - core) + (1 + r) // 2] = got[64 * n : 64 * n + 64].astype(BF)
    row_near.wait_recv()
    got = dot_nn(pick, snap[0])
    for n in range(3):
        xs[n, 0, 0] = got[64 * n : 64 * n + 64].astype(BF)
    for c in hcols:
        c.wait()
    tip_near.wait_recv()
    in_row = lax.broadcasted_iota(jnp.int32, (16, 256), 0)
    colv = jnp.where(rad == 1, cols_r[...].astype(F32), 0.0)
    corner = jnp.where(rad == 1, cols_c[...].astype(F32), 0.0)
    for e in range(33):
        tile = xs[0, e % 2, e // 2, 0:16, :].astype(F32)
        side = colv[e - 1 : e] if e else corner[15:16]
        xs[0, e % 2, e // 2, 0:16, :] = jnp.where(in_row == 0, side, tile).astype(BF)
    lw1.wait()
    f1 = []
    for d in (0, 2, 1):
        g1s[d].wait_recv()
    for d in (0, 2, 1):
        f1.append(hand_on(w1, d, every, 0))
    even = lax.rem(zlo, 2)

    def quarter(w, xi, taps):
        return w.at[taps, pl.ds(pl.multiple_of(64 * xi + 32 * core + 16 * even, 16), 16), :]

    g2s = {}
    for d in (0, 2, 1):
        g2s[d] = remote(
            w2_hbm.at[every, pl.ds(pl.multiple_of(32 * core + 16 * even, 16), 16), :],
            quarter(w2, x, every), wsend.at[3 + d], wrecv.at[3 + d], x_peers[d],
        )
        g2s[d].start()

    def edges(field, out):
        for r in range(16):
            edge(lambda c: field[r, c : c + 16, :], edgef, r)
        out[...] = edgef[...].astype(BF)

    def shifted(field, edge_got, sh):
        got = edge_got[...].astype(F32)
        for r in range(16):
            extf[r, 8:72, :] = field[r].astype(F32)
            part = got[4 * r : 4 * r + 4]
            extf[r, 4:8, :] = jnp.where(rad == 1, part, 0.0)
            extf[r, 72:76, :] = jnp.where(rad == 0, part, 0.0)
            sh[1, r] = field[r]
            sh[2, r] = extf[r, 4:68, :].astype(BF)
            sh[0, r] = extf[r, 12:76, :].astype(BF)

    def conv1(b, _):
        total = jnp.zeros((256, 128), F32)
        for t in range(9):
            m, n = t // 3, t % 3
            win = xs[n, m % 2, pl.ds(4 * b + m // 2, 4)].reshape(256, 256)
            w = jnp.concatenate(
                [w1[t, pl.ds(pl.multiple_of(64 * i + 32 * core, 32), 32), :] for i in range(4)], axis=0
            )
            total = total + dot_nt(win, w)
        sig = 1.0 / (1.0 + jnp.exp(-total))
        at[:, pl.ds(pl.multiple_of(256 * b, 256), 256)] = (total * sig).astype(BF).T
        return 0

    lax.fori_loop(0, 4, conv1, 0, unroll=True)
    def tiles_before(tile, k):
        q = tile // 9
        return sum((u // 4) % 2 == k for u in range(9 * q, tile))

    xc1 = []
    for chunk, taps in enumerate(((0, 1, 2), (3, 4), (5, 6), (7, 8))):
        for t in taps:
            m, n = t // 3, t % 3
            win = cot_sh[n, 8 - 4 * m : 24 - 4 * m].reshape(1024, 256)
            gt[t] = dot_nn(at[...], win) * (1.0 / 512.0)
        for k in range(2):
            @pl.when(core == k)
            def _():
                for tile in range(72 * chunk, 72 * chunk + 72):
                    if (tile // 4) % 2 != k:
                        continue
                    q, c = tile // 9, tiles_before(tile, k)
                    t, within = tile // 32, tile % 32
                    i = 4 * (within // 8) + within % 4
                    rows = gt[t, 8 * i : 8 * i + 8, :]
                    if c < 4:
                        g1[q % 4, 32 * (q // 4) + 8 * c : 32 * (q // 4) + 8 * c + 8, :] = rows
                    else:
                        g2[q // 4, 8 * (q % 4) : 8 * (q % 4) + 8, :] = rows
                for q in range(8 * chunk, 8 * chunk + 8):
                    if sum((u // 4) % 2 == k for u in range(9 * q, 9 * q + 9)) < 5:
                        g2[q // 4, 8 * (q % 4) : 8 * (q % 4) + 8, :] = jnp.zeros((8, 256), F32)

        some = slice(64 * chunk, 64 * chunk + 64)
        for i in range(4):
            xbuf1[i, some, :] = g1[i, some, :].astype(BF)
        for d in (1, 0, 2):
            c = remote(
                xbuf1.at[lax.rem(x + 1 + d, 4), pl.ds(64 * chunk, 64)], xr1.at[d, pl.ds(64 * chunk, 64)],
                xss.at[3 * chunk + d], xrs.at[3 * chunk + d], x_peers[d],
            )
            c.start()
            xc1.append(c)
    for i in range(8):
        ybuf2[i] = g2[i].astype(BF)
    yc2 = []
    for d in (3, 2, 4, 1, 5, 0, 6):
        c = remote(ybuf2.at[lax.rem(y + 1 + d, 8)], yr2.at[d], yss.at[d], yrs.at[d], y_peers[d])
        c.start()
        yc2.append(c)

    for c in f1:
        c.wait()
    for d in range(3):
        g1s[d].wait_send()

    def own(b, _):
        at_row = 4 * b
        total = jnp.zeros((256, 256), F32)
        for t in range(9):
            m, n = t // 3, t % 3
            win = xs[n, m % 2, pl.ds(8 * core + at_row + m // 2, 4)].reshape(256, 256)
            total = total + dot_nt(win, w1[t])
        pre[pl.ds(pl.multiple_of(256 * b, 256), 256), :] = total
        sig = 1.0 / (1.0 + jnp.exp(-total))
        actr[pl.ds(4 + at_row, 4)] = (total * sig).astype(BF).reshape(4, 64, 256)
        return 0

    lax.fori_loop(0, 2, own, 0)
    hact_u = remote(actr.at[4:8], actr.at[12:16], hs.at[16], hr.at[16], up)
    hact_u.start()
    hact_d = remote(actr.at[8:12], actr.at[0:4], hs.at[19], hr.at[19], down)
    hact_d.start()
    by_z = []
    for d in (0, 2, 1):
        g2s[d].wait_recv()
        for i, (taps, target) in enumerate(((pl.ds(0, 5), z_next), (pl.ds(5, 4), z_prev))):
            part = quarter(w2, lax.rem(x + 3 - d, 4), taps)
            c = remote(part, part, wzs.at[2 * d + i], wzr.at[2 * d + i], target)
            c.start()
            by_z.append(c)
    f2 = []
    for i, d in enumerate((0, 2, 1)):
        by_z[2 * i].wait_recv()
        by_z[2 * i + 1].wait_recv()
        f2.append(hand_on(w2, d, every, 3))
    lw2.wait()

    yc1 = []
    for chunk in range(4):
        for c in xc1[3 * chunk : 3 * chunk + 3]:
            c.wait()
        for j in (2 * chunk, 2 * chunk + 1):
            rows = slice(32 * j, 32 * j + 32)
            s = g1[x, rows, :]
            for d in range(3):
                s = s + xr1[d, rows, :].astype(F32)
            s1[j] = s
            ybuf1[j] = s.astype(BF)
            d = lax.rem(j + 7 - y + 8, 8)

            @pl.when(y != j)
            def _():
                remote(
                    ybuf1.at[j], yr1.at[d], yss.at[7 + d], yrs.at[7 + d], dev(j * 8 + zlo * 2 + core, rad, x)
                ).start()
    for d in range(7):
        yc1.append(remote(ybuf1.at[0], yr1.at[d], yss.at[7 + d], yrs.at[7 + d], y_peers[d]))
    for c in yc2:
        c.wait()
    s = g2[y]
    for d in range(7):
        s = s + yr2[d].astype(F32)
    for i in range(4):
        s2[i, 0:8, :] = s[8 * i : 8 * i + 8]
        s2[i, 8:16, :] = jnp.zeros((8, 256), F32)
    for i in range(4):
        xbuf2[i] = s2[i].astype(BF)
    xc2 = []
    for d in (1, 0, 2):
        c = remote(xbuf2.at[lax.rem(x + 1 + d, 4)], xr2.at[d], xss.at[12 + d], xrs.at[12 + d], x_peers[d])
        c.start()
        xc2.append(c)

    hact_d.wait()
    hact_u.wait()
    edges(actr, aedge_s)
    haedge = remote(aedge_s, aedge_r, hs.at[9], hr.at[9], band)
    haedge.start()
    for d in range(3):
        f2[d].wait()
        g2s[d].wait_send()
        by_z[2 * d].wait_send()
        by_z[2 * d + 1].wait_send()

    def back(b, _):
        at_row = 4 * b
        cells = pl.ds(pl.multiple_of(256 * b, 256), 256)
        total = cot24[pl.ds(4 + 8 * core + at_row, 4)].reshape(256, 256).astype(F32)
        for t in range(9):
            m, n = t // 3, t % 3
            win = cot_sh[n, pl.ds(8 * core + at_row + 8 - 4 * m, 4)].reshape(256, 256)
            total = total + dot_nn(win, w2[t])
        v = pre[cells, :]
        s = 1.0 / (1.0 + jnp.exp(-v))
        g = (total * (s * (1.0 + v * (1.0 - s)))).astype(BF)
        gp[pl.ds(at_row, 4)] = g.reshape(4, 64, 256)
        for i in range(4):
            colf[pl.ds(at_row + i, 1), :] = g[64 * i : 64 * i + 16].astype(F32)[0:1]
        return 0

    lax.fori_loop(0, 2, back, 0)
    gcol_s[...] = colf[0:16, :].astype(BF)
    hgp = [
        remote(gp.at[0], gp.at[8], hs.at[10], hr.at[10], up),
        remote(gcol_s, gcol_r, hs.at[11], hr.at[11], band),
        remote(gcol_s, gcol_c, hs.at[17], hr.at[17], across(up)),
    ]
    for c in hgp:
        c.start()

    for c in xc2:
        c.wait()
    s = s2[x]
    for d in range(3):
        s = s + xr2[d].astype(F32)
    zcom[4] = s[0:8]
    for c in yc1:
        c.wait()
    s = s1[y]
    for d in range(7):
        s = s + yr1[d].astype(F32)
    for i in range(4):
        zcom[i] = s[8 * i : 8 * i + 8]
    phase = lax.rem(4 * y + x, 8)
    before = 0
    for u in range(9):
        held = lax.rem((phase + u) // 4, 2) == core
        tile = zcom[before if u == 0 else jnp.minimum(before, 4)]
        zsum[8 * u : 8 * u + 8, :] = jnp.where(held, tile, 0.0)
        before = before + jnp.where(held, 1, 0)
    zsum[72:80, :] = jnp.zeros((8, 256), F32)
    for p in range(16):
        rows = zsum[(9 * p) // 2 : (9 * p) // 2 + 8, :]
        pbuf[p] = jnp.concatenate([rows[:, 0:128], rows[:, 128:256]], axis=0).astype(BF)
    slot = core * 8 + rad * 4 + zlo
    zc = []
    for p in range(16):
        c1, zh, xp = p // 8, (p // 4) % 2, p % 4
        is_self = own_home & (core == c1) & (rad == zh) & (x == xp)
        rc = remote(pbuf.at[p], prec.at[slot], zss.at[p], zrs.at[slot], dev((y * 4 + x) * 2 + c1, zh, xp))
        lc = pltpu.make_async_copy(pbuf.at[p], prec.at[slot], zrs.at[slot])

        @pl.when(is_self)
        def _():
            lc.start()

        @pl.when(jnp.logical_not(is_self))
        def _():
            rc.start()

        zc.append((is_self, rc))

    haedge.wait()
    shifted(actr, aedge_r, act_sh)

    def ahead(b, _):
        at_row = 4 * b
        total = act_sh[1, pl.ds(4 + at_row, 4)].reshape(256, 256).astype(F32)
        for t in range(9):
            m, n = t // 3, t % 3
            win = act_sh[2 - n, pl.ds(at_row + 4 * m, 4)].reshape(256, 256)
            total = total + dot_nt(win, w2[t])
        enc_ref[pl.ds(at_row, 4)] = total.astype(BF).reshape(4, 64, 256)
        return 0

    lax.fori_loop(0, 2, ahead, 0)
    for c in hgp:
        c.wait()
    colv = jnp.where(rad == 0, gcol_r[...].astype(F32), 0.0)
    corner = jnp.where(rad == 0, gcol_c[...].astype(F32), 0.0)
    for r in range(9):
        gpf[r, 0:64, :] = gp[r].astype(F32)
        gpf[r, 64:65, :] = colv[r : r + 1] if r < 8 else corner[0:1]
        gp1[r] = gpf[r, 1:65, :].astype(BF)

    row_q = lax.broadcasted_iota(jnp.int32, (128, 128), 0)
    col_q = lax.broadcasted_iota(jnp.int32, (128, 128), 1)
    weave = jnp.where(col_q == lax.rem(row_q, 2) * 64 + row_q // 2, 1.0, 0.0).astype(BF)
    ptaps = (((1, 0),), ((2, 0), (0, 1)))

    def inward(b, _):
        at_row = 4 * b
        for rp in range(2):
            halves = []
            for cp in range(2):
                total = jnp.zeros((256, 256), F32)
                for m, rs in ptaps[rp]:
                    for n, cs in ptaps[cp]:
                        field = gp1 if cs else gp
                        win = field[pl.ds(at_row + rs, 4)].reshape(256, 256)
                        total = total + dot_nn(win, w1[3 * m + n])
                halves.append(total.astype(BF).reshape(4, 64, 256))
            for i in range(4):
                pair = jnp.concatenate([halves[0][i], halves[1][i]], axis=0)
                ing_ref[2 * (at_row + i) + rp] = dot_nn(weave, pair).astype(BF)
        return 0

    lax.fori_loop(0, 2, inward, 0)
    @pl.when(core == 1)
    def _():
        for c in (row_near, row_far, tip_near, tip_far):
            c.wait_send()


    for s in range(16):
        pltpu.make_async_copy(pbuf.at[0], prec.at[s], zrs.at[s]).wait()
    s = prec[0].astype(F32)
    for i in range(1, 16):
        s = s + prec[i].astype(F32)
    for i in range(5):
        fin[2 * i : 2 * i + 1, :] = s[i : i + 1]
        fin[2 * i + 1 : 2 * i + 2, :] = s[8 + i : 9 + i]
    result = jnp.where(lax.rem(x, 2) == 0, fin[0:9, :], fin[1:10, :])
    for i in range(9):
        kg_ref[128 * i : 128 * i + 128] = result[i]
    for is_self, rc in zc:
        @pl.when(jnp.logical_not(is_self))
        def _():
            rc.wait_send()


def closing(enc_in, ing_in, kg_in, enc_out, ing_out, kg_out, sem):
    copies = [
        pltpu.make_async_copy(src, dst, sem.at[i])
        for i, (src, dst) in enumerate(((ing_in, ing_out), (enc_in, enc_out), (kg_in, kg_out)))
    ]
    for c in copies:
        c.start()
    for c in copies:
        c.wait()


def body(snapshots, first_kernel, second_kernel, cotangent):
    def vm(shape, kind=BF):
        return pltpu.VMEM(shape, kind)

    dma = pltpu.SemaphoreType.DMA
    scratch = [
        vm((33, 128, 256)), vm((3, 2, 17, 64, 256)), vm((40, 256), F32), vm((16, 256)), vm((32, 256)), vm((16, 256)),
        vm((9, 256, 256)), vm((9, 256, 256)), vm((24, 64, 256)), vm((3, 24, 64, 256)),
        vm((64, 256), F32), vm((32, 256)), vm((96, 256)), vm((64, 256)), vm((64, 256)),
        vm((24, 80, 256), F32), vm((16, 64, 256)),
        vm((3, 16, 64, 256)), vm((512, 256), F32), vm((128, 1024)), vm((9, 128, 256), F32),
        vm((4, 256, 256), F32), vm((8, 32, 256), F32), vm((4, 256, 256)), vm((3, 256, 256)),
        vm((8, 32, 256), F32), vm((8, 32, 256)), vm((7, 32, 256)), vm((8, 32, 256)), vm((7, 32, 256)),
        vm((4, 16, 256), F32), vm((4, 16, 256)), vm((3, 16, 256)),
        vm((5, 8, 256), F32), vm((80, 256), F32), vm((16, 16, 128)), vm((16, 16, 128)), vm((16, 128), F32),
        vm((9, 64, 256)), vm((9, 64, 256)), vm((9, 80, 256), F32), vm((16, 256)), vm((16, 256)), vm((16, 256)),
        dma((4,)), dma((6,)), dma((6,)), dma((6,)), dma((6,)), dma((6,)), dma((6,)), dma((20,)), dma((20,)),
        dma((15,)), dma((15,)), dma((14,)), dma((14,)), dma((16,)), dma((16,)),
    ]
    enc, ing, kg = pl.pallas_call(
        kernel,
        name="section",
        out_shape=(
            pltpu.VMEM((8, 64, 256), BF),
            pltpu.VMEM((16, 128, 256), BF),
            pltpu.VMEM((1152,), F32),
        ),
        in_specs=[pl.BlockSpec(memory_space=pl.ANY)] * 4,
        out_specs=[pl.BlockSpec(memory_space=pltpu.VMEM)] * 3,
        scratch_shapes=scratch,
        compiler_params=pltpu.CompilerParams(
            collective_id=0, has_side_effects=True, vmem_limit_bytes=56 << 20
        ),
    )(
        snapshots[0],
        jnp.swapaxes(first_kernel, 1, 2),
        jnp.swapaxes(second_kernel, 1, 2),
        cotangent[0],
    )
    enc, ing, kg = pl.pallas_call(
        closing,
        name="closing",
        out_shape=(
            jax.ShapeDtypeStruct((8, 64, 256), BF),
            jax.ShapeDtypeStruct((16, 128, 256), BF),
            jax.ShapeDtypeStruct((1152,), F32),
        ),
        in_specs=[pl.BlockSpec(memory_space=pl.ANY)] * 3,
        out_specs=[pl.BlockSpec(memory_space=pl.ANY)] * 3,
        scratch_shapes=[dma((3,))],
        compiler_params=pltpu.CompilerParams(vmem_limit_bytes=1 << 20),
    )(enc, ing, kg)
    return enc[None], ing[None], kg


def solution(mesh):
    return jax.shard_map(
        body,
        mesh=mesh,
        in_specs=(
            P("batch", "azi", "rad", None),
            P(None, None, "batch"),
            P(None, None, "batch"),
            P("batch", "azi", "rad", None),
        ),
        out_specs=(
            P("batch", "azi", "rad", None),
            P("batch", "azi", "rad", None),
            P(("azi", "rad", "batch")),
        ),
        check_vma=False,
    )
```

```python
import jax
import jax.numpy as jnp
from jax import lax
from jax.experimental import pallas as pl
from jax.experimental.pallas import tpu as pltpu
from jax.sharding import PartitionSpec as P

BF = jnp.bfloat16
F32 = jnp.float32
SHIFTS = (4, 0, -4)


def dot_nt(a, b):
    return lax.dot_general(a, b, (((1,), (1,)), ((), ())), preferred_element_type=F32)


def dot_nn(a, b):
    return lax.dot_general(a, b, (((1,), (0,)), ((), ())), preferred_element_type=F32)


def kernel(
    snap_hbm, w1_hbm, w2_hbm, cot_hbm,
    enc_ref, ing_ref, kg_ref,
    snap, xs, colf, cols_s, cols_r, cols_c, w1, w2, cot24, cot_sh, edgef, cedge_s, cedge_r, aedge_s, aedge_r,
    extf, actr, act_sh, pre, at, gt, g1, g2, xbuf1, xr1, s1, ybuf1, yr1, ybuf2, yr2, s2, xbuf2, xr2,
    zcom, zsum, pbuf, prec, fin, gp, gp1, gpf, gcol_s, gcol_r, gcol_c,
    loc_sem, wsend, wrecv, wfs, wfr, wzs, wzr, hs, hr, xss, xrs, yss, yrs, zss, zrs,
):
    a = lax.axis_index("azi")
    rad = lax.axis_index("rad")
    x = lax.axis_index("batch")
    core = lax.rem(a, 2)
    zlo = lax.rem(a // 2, 4)
    y = a // 8

    def dev(azi, r, b):
        return {"azi": azi, "rad": r, "batch": b}

    def signal(target):
        pl.semaphore_signal(barrier, inc=1, device_id=target, device_id_type=pl.DeviceIdType.MESH)

    def remote(src, dst, ss, rs, target):
        return pltpu.make_async_remote_copy(
            src_ref=src, dst_ref=dst, send_sem=ss, recv_sem=rs,
            device_id=target, device_id_type=pl.DeviceIdType.MESH,
        )

    other = dev(a + 1 - 2 * core, rad, x)
    up = dev(lax.rem(a + 63, 64), rad, x)
    down = dev(lax.rem(a + 1, 64), rad, x)
    band = dev(a, 1 - rad, x)
    step = 2 * core - 1
    near = dev(lax.rem(a + 64 + step, 64), rad, x)

    zi = 4 * rad + zlo

    def along_z(by):
        z2 = lax.rem(zi + 8 + by, 8)
        return dev(y * 8 + lax.rem(z2, 4) * 2 + core, z2 // 4, x)

    z_next, z_prev = along_z(1), along_z(-1)

    def across(target):
        return dev(target["azi"], 1 - rad, x)

    x_peers = [dev(a, rad, lax.rem(x + d, 4)) for d in (1, 2, 3)]
    y_peers = [dev(lax.rem(y + d, 8) * 8 + zlo * 2 + core, rad, x) for d in range(1, 8)]
    own_home = zlo == x

    barrier = pltpu.get_barrier_semaphore()
    for target in [other, up, down, band, across(near), across(up), across(down), z_next, z_prev] + x_peers + y_peers:
        signal(target)
    for cs in range(2):
        for zh in range(2):
            for zl in range(4):
                is_self = own_home & (core == cs) & (rad == zh) & (zlo == zl)

                @pl.when(jnp.logical_not(is_self))
                def _():
                    signal(dev((y * 4 + zl) * 2 + cs, zh, zlo))

    def shard_rows(w):
        return w.at[:, pl.ds(pl.multiple_of(64 * x, 64), 64), :]

    def half_rows(w, xi, k):
        return w.at[:, pl.ds(pl.multiple_of(64 * xi + 32 * k, 32), 32), :]

    own_snap = pl.ds(1 + 16 * core, 16)
    lsnap = pltpu.make_async_copy(snap_hbm, snap.at[own_snap], loc_sem.at[0])
    lw1 = pltpu.make_async_copy(w1_hbm, shard_rows(w1), loc_sem.at[1])
    lw2 = pltpu.make_async_copy(w2_hbm, shard_rows(w2), loc_sem.at[2])
    own_rows = pl.ds(4 + 8 * core, 8)
    lcot = pltpu.make_async_copy(cot_hbm, cot24.at[own_rows], loc_sem.at[3])
    for c in (lcot, lsnap, lw1, lw2):
        c.start()

    def edge(tile_of, out, r):
        low = tile_of(0).astype(F32)[0:4]
        high = tile_of(48).astype(F32)[12:16]
        out[4 * r : 4 * r + 4, :] = jnp.where(rad == 0, high, low)

    lcot.wait()
    for r in range(8):
        edge(lambda c: cot24[4 + 8 * core + r, c : c + 16, :], edgef, r)
    cedge_s[...] = edgef[0:32, :].astype(BF)
    pl.semaphore_wait(barrier, jnp.where(own_home, 34, 35))

    base = pl.ds(pl.multiple_of(32 * core, 32), 32)

    def part_of(w, xi, taps, k):
        return w.at[taps, pl.ds(pl.multiple_of(64 * xi + 32 * k, 32), 32), :]

    def gather_send(w, w_hbm, taps, at_sem):
        out = {}
        for d in (0, 2, 1):
            out[d] = remote(
                w_hbm.at[taps, base, :], part_of(w, x, taps, core), wsend.at[at_sem + d], wrecv.at[at_sem + d], x_peers[d]
            )
            out[d].start()
        return out

    def hand_on(w, d, taps, at_sem):
        part = part_of(w, lax.rem(x + 3 - d, 4), taps, core)
        c = remote(part, part, wfs.at[at_sem + d], wfr.at[at_sem + d], other)
        c.start()
        return c

    every = pl.ds(0, 9)
    g1s = gather_send(w1, w1_hbm, every, 0)
    hsnap = remote(snap_hbm, snap.at[own_snap], hs.at[0], hr.at[0], other)
    hsnap.start()
    row_near = remote(snap_hbm.at[15], snap.at[0], hs.at[6], hr.at[6], near)
    row_pass = remote(snap.at[0], snap.at[0], hs.at[7], hr.at[7], other)

    @pl.when(core == 1)
    def _():
        row_near.start()

    edge_rows = pl.ds(4 * core, 4)
    far_rows = pl.ds(20 * (1 - core), 4)
    mid = pl.ds(pl.multiple_of(16 + 32 * core, 16), 32)
    tip = pl.ds(pl.multiple_of(80 * (1 - core), 16), 16)
    tip_s = pl.ds(pl.multiple_of(16 * core, 16), 16)
    cot_halo = [
        remote(cot_hbm.at[edge_rows], cot24.at[far_rows], hs.at[1], hr.at[1], near),
        remote(cedge_s, cedge_r.at[mid], hs.at[12], hr.at[12], band),
        remote(cedge_s.at[tip_s], cedge_r.at[tip], hs.at[14], hr.at[14], across(near)),
        remote(cot_hbm, cot24.at[own_rows], hs.at[4], hr.at[4], other),
    ]
    for c in cot_halo:
        c.start()
    got_rows = cot24.at[pl.ds(20 * core, 4)]
    got_tip = cedge_r.at[pl.ds(pl.multiple_of(80 * core, 16), 16)]
    cot_pass = [
        remote(got_rows, got_rows, hs.at[2], hr.at[2], other),
        remote(cedge_r.at[mid], cedge_r.at[mid], hs.at[13], hr.at[13], other),
        remote(got_tip, got_tip, hs.at[15], hr.at[15], other),
    ]

    row_i = lax.broadcasted_iota(jnp.int32, (192, 128), 0)
    col_i = lax.broadcasted_iota(jnp.int32, (192, 128), 1)
    pick = jnp.where(col_i == 2 * lax.rem(row_i, 64) + row_i // 64 - 1, 1.0, 0.0).astype(BF)

    lsnap.wait()
    for r in range(16):
        e = 16 * core + 1 + r
        got = dot_nn(pick, snap[e])
        for n in range(3):
            xs[n, (1 + r) % 2, 8 * core + (1 + r) // 2] = got[64 * n : 64 * n + 64].astype(BF)
        colf[r : r + 1, :] = got[191:192]
    cols_s[...] = colf[0:16, :].astype(BF)
    col_rows = pl.ds(pl.multiple_of(16 * core, 16), 16)
    hcols = remote(cols_s, cols_r.at[col_rows], hs.at[3], hr.at[3], band)
    hcols.start()
    cols_pass = remote(cols_r.at[col_rows], cols_r.at[col_rows], hs.at[5], hr.at[5], other)
    tip_near = remote(cols_s, cols_c, hs.at[8], hr.at[8], across(near))
    tip_pass = remote(cols_c, cols_c, hs.at[18], hr.at[18], other)

    @pl.when(core == 1)
    def _():
        tip_near.start()

    hsnap.wait()
    for r in range(16):
        e = 16 * (1 - core) + 1 + r
        got = dot_nn(pick, snap[e])
        for n in range(3):
            xs[n, (1 + r) % 2, 8 * (1 - core) + (1 + r) // 2] = got[64 * n : 64 * n + 64].astype(BF)
    for d in (0, 2, 1):
        g1s[d].wait_recv()
    even = lax.rem(zlo, 2)

    def quarter(w, xi, taps):
        return w.at[taps, pl.ds(pl.multiple_of(64 * xi + 32 * core + 16 * even, 16), 16), :]

    g2s = {}
    for d in (0, 2, 1):
        g2s[d] = remote(
            w2_hbm.at[every, pl.ds(pl.multiple_of(32 * core + 16 * even, 16), 16), :],
            quarter(w2, x, every), wsend.at[3 + d], wrecv.at[3 + d], x_peers[d],
        )
        g2s[d].start()

    @pl.when(core == 0)
    def _():
        row_near.wait_recv()
        row_pass.start()
        tip_near.wait_recv()
        tip_pass.start()

    hcols.wait()
    cols_pass.start()
    for i in range(3):
        cot_halo[i].wait_recv()
        cot_pass[i].start()
    f1 = []
    for d in (0, 2, 1):
        f1.append(hand_on(w1, d, every, 0))

    @pl.when(core == 1)
    def _():
        row_pass.wait_recv()
        tip_pass.wait_recv()
        row_near.wait_send()
        tip_near.wait_send()

    got = dot_nn(pick, snap[0])
    for n in range(3):
        xs[n, 0, 0] = got[64 * n : 64 * n + 64].astype(BF)
    cols_pass.wait()
    in_row = lax.broadcasted_iota(jnp.int32, (16, 256), 0)
    colv = jnp.where(rad == 1, cols_r[...].astype(F32), 0.0)
    corner = jnp.where(rad == 1, cols_c[...].astype(F32), 0.0)
    for e in range(33):
        tile = xs[0, e % 2, e // 2, 0:16, :].astype(F32)
        side = colv[e - 1 : e] if e else corner[15:16]
        xs[0, e % 2, e // 2, 0:16, :] = jnp.where(in_row == 0, side, tile).astype(BF)
    lw1.wait()

    def edges(field, out):
        for r in range(16):
            edge(lambda c: field[r, c : c + 16, :], edgef, r)
        out[...] = edgef[...].astype(BF)

    def shifted(field, edge_got, sh):
        got = edge_got[...].astype(F32)
        for r in range(16):
            extf[r, 8:72, :] = field[r].astype(F32)
            part = got[4 * r : 4 * r + 4]
            extf[r, 4:8, :] = jnp.where(rad == 1, part, 0.0)
            extf[r, 72:76, :] = jnp.where(rad == 0, part, 0.0)
            sh[1, r] = field[r]
            sh[2, r] = extf[r, 4:68, :].astype(BF)
            sh[0, r] = extf[r, 12:76, :].astype(BF)

    def conv1(b, _):
        total = jnp.zeros((256, 128), F32)
        for t in range(9):
            m, n = t // 3, t % 3
            win = xs[n, m % 2, pl.ds(4 * b + m // 2, 4)].reshape(256, 256)
            w = jnp.concatenate(
                [w1[t, pl.ds(pl.multiple_of(64 * i + 32 * core, 32), 32), :] for i in range(4)], axis=0
            )
            total = total + dot_nt(win, w)
        sig = 1.0 / (1.0 + jnp.exp(-total))
        at[:, pl.ds(pl.multiple_of(256 * b, 256), 256)] = (total * sig).astype(BF).T
        return 0

    lax.fori_loop(0, 4, conv1, 0, unroll=True)

    for c in cot_pass:
        c.wait()
    cot_halo[3].wait()
    for c in cot_halo[0:3]:
        c.wait_send()
    got = cedge_r[...].astype(F32)
    for r in range(24):
        extf[r, 8:72, :] = cot24[r].astype(F32)
        part = got[4 * r : 4 * r + 4]
        extf[r, 4:8, :] = jnp.where(rad == 1, part, 0.0)
        extf[r, 72:76, :] = jnp.where(rad == 0, part, 0.0)
        for n, start in ((0, 12), (1, 8), (2, 4)):
            cot_sh[n, r] = extf[r, start : start + 64, :].astype(BF)

    def tiles_before(tile, k):
        q = tile // 9
        return sum((u // 4) % 2 == k for u in range(9 * q, tile))

    xc1 = []
    for chunk, taps in enumerate(((0, 1, 2), (3, 4), (5, 6), (7, 8))):
        for t in taps:
            m, n = t // 3, t % 3
            win = cot_sh[n, 8 - 4 * m : 24 - 4 * m].reshape(1024, 256)
            gt[t] = dot_nn(at[...], win) * (1.0 / 512.0)
        for k in range(2):
            @pl.when(core == k)
            def _():
                for tile in range(72 * chunk, 72 * chunk + 72):
                    if (tile // 4) % 2 != k:
                        continue
                    q, c = tile // 9, tiles_before(tile, k)
                    t, within = tile // 32, tile % 32
                    i = 4 * (within // 8) + within % 4
                    rows = gt[t, 8 * i : 8 * i + 8, :]
                    if c < 4:
                        g1[q % 4, 32 * (q // 4) + 8 * c : 32 * (q // 4) + 8 * c + 8, :] = rows
                    else:
                        g2[q // 4, 8 * (q % 4) : 8 * (q % 4) + 8, :] = rows
                for q in range(8 * chunk, 8 * chunk + 8):
                    if sum((u // 4) % 2 == k for u in range(9 * q, 9 * q + 9)) < 5:
                        g2[q // 4, 8 * (q % 4) : 8 * (q % 4) + 8, :] = jnp.zeros((8, 256), F32)

        some = slice(64 * chunk, 64 * chunk + 64)
        for i in range(4):
            xbuf1[i, some, :] = g1[i, some, :].astype(BF)
        for d in (1, 0, 2):
            c = remote(
                xbuf1.at[lax.rem(x + 1 + d, 4), pl.ds(64 * chunk, 64)], xr1.at[d, pl.ds(64 * chunk, 64)],
                xss.at[3 * chunk + d], xrs.at[3 * chunk + d], x_peers[d],
            )
            c.start()
            xc1.append(c)
    for i in range(8):
        ybuf2[i] = g2[i].astype(BF)
    yc2 = []
    for d in (3, 2, 4, 1, 5, 0, 6):
        c = remote(ybuf2.at[lax.rem(y + 1 + d, 8)], yr2.at[d], yss.at[d], yrs.at[d], y_peers[d])
        c.start()
        yc2.append(c)

    for c in f1:
        c.wait()
    for d in range(3):
        g1s[d].wait_send()

    def own(b, _):
        at_row = 4 * b
        total = jnp.zeros((256, 256), F32)
        for t in range(9):
            m, n = t // 3, t % 3
            win = xs[n, m % 2, pl.ds(8 * core + at_row + m // 2, 4)].reshape(256, 256)
            total = total + dot_nt(win, w1[t])
        pre[pl.ds(pl.multiple_of(256 * b, 256), 256), :] = total
        sig = 1.0 / (1.0 + jnp.exp(-total))
        actr[pl.ds(4 + at_row, 4)] = (total * sig).astype(BF).reshape(4, 64, 256)
        return 0

    lax.fori_loop(0, 2, own, 0)
    hact_u = remote(actr.at[4:8], actr.at[12:16], hs.at[16], hr.at[16], up)
    hact_u.start()
    hact_d = remote(actr.at[8:12], actr.at[0:4], hs.at[19], hr.at[19], down)
    hact_d.start()
    by_z = []
    for d in (0, 2, 1):
        g2s[d].wait_recv()
        for i, (taps, target) in enumerate(((pl.ds(0, 5), z_next), (pl.ds(5, 4), z_prev))):
            part = quarter(w2, lax.rem(x + 3 - d, 4), taps)
            c = remote(part, part, wzs.at[2 * d + i], wzr.at[2 * d + i], target)
            c.start()
            by_z.append(c)
    f2 = []
    for i, d in enumerate((0, 2, 1)):
        by_z[2 * i].wait_recv()
        by_z[2 * i + 1].wait_recv()
        f2.append(hand_on(w2, d, every, 3))
    lw2.wait()

    yc1 = []
    for chunk in range(4):
        for c in xc1[3 * chunk : 3 * chunk + 3]:
            c.wait()
        for j in (2 * chunk, 2 * chunk + 1):
            rows = slice(32 * j, 32 * j + 32)
            s = g1[x, rows, :]
            for d in range(3):
                s = s + xr1[d, rows, :].astype(F32)
            s1[j] = s
            ybuf1[j] = s.astype(BF)
            d = lax.rem(j + 7 - y + 8, 8)

            @pl.when(y != j)
            def _():
                remote(
                    ybuf1.at[j], yr1.at[d], yss.at[7 + d], yrs.at[7 + d], dev(j * 8 + zlo * 2 + core, rad, x)
                ).start()
    for d in range(7):
        yc1.append(remote(ybuf1.at[0], yr1.at[d], yss.at[7 + d], yrs.at[7 + d], y_peers[d]))
    for c in yc2:
        c.wait()
    s = g2[y]
    for d in range(7):
        s = s + yr2[d].astype(F32)
    for i in range(4):
        s2[i, 0:8, :] = s[8 * i : 8 * i + 8]
        s2[i, 8:16, :] = jnp.zeros((8, 256), F32)
    for i in range(4):
        xbuf2[i] = s2[i].astype(BF)
    xc2 = []
    for d in (1, 0, 2):
        c = remote(xbuf2.at[lax.rem(x + 1 + d, 4)], xr2.at[d], xss.at[12 + d], xrs.at[12 + d], x_peers[d])
        c.start()
        xc2.append(c)

    hact_d.wait()
    hact_u.wait()
    edges(actr, aedge_s)
    haedge = remote(aedge_s, aedge_r, hs.at[9], hr.at[9], band)
    haedge.start()
    for d in range(3):
        f2[d].wait()
        g2s[d].wait_send()
        by_z[2 * d].wait_send()
        by_z[2 * d + 1].wait_send()

    def back(b, _):
        at_row = 4 * b
        cells = pl.ds(pl.multiple_of(256 * b, 256), 256)
        total = cot24[pl.ds(4 + 8 * core + at_row, 4)].reshape(256, 256).astype(F32)
        for t in range(9):
            m, n = t // 3, t % 3
            win = cot_sh[n, pl.ds(8 * core + at_row + 8 - 4 * m, 4)].reshape(256, 256)
            total = total + dot_nn(win, w2[t])
        v = pre[cells, :]
        s = 1.0 / (1.0 + jnp.exp(-v))
        g = (total * (s * (1.0 + v * (1.0 - s)))).astype(BF)
        gp[pl.ds(at_row, 4)] = g.reshape(4, 64, 256)
        for i in range(4):
            colf[pl.ds(at_row + i, 1), :] = g[64 * i : 64 * i + 16].astype(F32)[0:1]
        return 0

    lax.fori_loop(0, 2, back, 0)
    gcol_s[...] = colf[0:16, :].astype(BF)
    hgp = [
        remote(gp.at[0], gp.at[8], hs.at[10], hr.at[10], up),
        remote(gcol_s, gcol_r, hs.at[11], hr.at[11], band),
        remote(gcol_s, gcol_c, hs.at[17], hr.at[17], across(up)),
    ]
    for c in hgp:
        c.start()

    for c in xc2:
        c.wait()
    s = s2[x]
    for d in range(3):
        s = s + xr2[d].astype(F32)
    zcom[4] = s[0:8]
    for c in yc1:
        c.wait()
    s = s1[y]
    for d in range(7):
        s = s + yr1[d].astype(F32)
    for i in range(4):
        zcom[i] = s[8 * i : 8 * i + 8]
    phase = lax.rem(4 * y + x, 8)
    before = 0
    for u in range(9):
        held = lax.rem((phase + u) // 4, 2) == core
        tile = zcom[before if u == 0 else jnp.minimum(before, 4)]
        zsum[8 * u : 8 * u + 8, :] = jnp.where(held, tile, 0.0)
        before = before + jnp.where(held, 1, 0)
    zsum[72:80, :] = jnp.zeros((8, 256), F32)
    for p in range(16):
        rows = zsum[(9 * p) // 2 : (9 * p) // 2 + 8, :]
        pbuf[p] = jnp.concatenate([rows[:, 0:128], rows[:, 128:256]], axis=0).astype(BF)
    slot = core * 8 + rad * 4 + zlo
    zc = []
    for p in range(16):
        c1, zh, xp = p // 8, (p // 4) % 2, p % 4
        is_self = own_home & (core == c1) & (rad == zh) & (x == xp)
        rc = remote(pbuf.at[p], prec.at[slot], zss.at[p], zrs.at[slot], dev((y * 4 + x) * 2 + c1, zh, xp))
        lc = pltpu.make_async_copy(pbuf.at[p], prec.at[slot], zrs.at[slot])

        @pl.when(is_self)
        def _():
            lc.start()

        @pl.when(jnp.logical_not(is_self))
        def _():
            rc.start()

        zc.append((is_self, rc))

    haedge.wait()
    shifted(actr, aedge_r, act_sh)

    def ahead(b, _):
        at_row = 4 * b
        total = act_sh[1, pl.ds(4 + at_row, 4)].reshape(256, 256).astype(F32)
        for t in range(9):
            m, n = t // 3, t % 3
            win = act_sh[2 - n, pl.ds(at_row + 4 * m, 4)].reshape(256, 256)
            total = total + dot_nt(win, w2[t])
        enc_ref[pl.ds(at_row, 4)] = total.astype(BF).reshape(4, 64, 256)
        return 0

    lax.fori_loop(0, 2, ahead, 0)
    for c in hgp:
        c.wait()
    colv = jnp.where(rad == 0, gcol_r[...].astype(F32), 0.0)
    corner = jnp.where(rad == 0, gcol_c[...].astype(F32), 0.0)
    for r in range(9):
        gpf[r, 0:64, :] = gp[r].astype(F32)
        gpf[r, 64:65, :] = colv[r : r + 1] if r < 8 else corner[0:1]
        gp1[r] = gpf[r, 1:65, :].astype(BF)

    row_q = lax.broadcasted_iota(jnp.int32, (128, 128), 0)
    col_q = lax.broadcasted_iota(jnp.int32, (128, 128), 1)
    weave = jnp.where(col_q == lax.rem(row_q, 2) * 64 + row_q // 2, 1.0, 0.0).astype(BF)
    ptaps = (((1, 0),), ((2, 0), (0, 1)))

    def inward(b, _):
        at_row = 4 * b
        for rp in range(2):
            halves = []
            for cp in range(2):
                total = jnp.zeros((256, 256), F32)
                for m, rs in ptaps[rp]:
                    for n, cs in ptaps[cp]:
                        field = gp1 if cs else gp
                        win = field[pl.ds(at_row + rs, 4)].reshape(256, 256)
                        total = total + dot_nn(win, w1[3 * m + n])
                halves.append(total.astype(BF).reshape(4, 64, 256))
            for i in range(4):
                pair = jnp.concatenate([halves[0][i], halves[1][i]], axis=0)
                ing_ref[2 * (at_row + i) + rp] = dot_nn(weave, pair).astype(BF)
        return 0

    lax.fori_loop(0, 2, inward, 0)

    @pl.when(core == 0)
    def _():
        row_pass.wait_send()
        tip_pass.wait_send()


    for s in range(16):
        pltpu.make_async_copy(pbuf.at[0], prec.at[s], zrs.at[s]).wait()
    s = prec[0].astype(F32)
    for i in range(1, 16):
        s = s + prec[i].astype(F32)
    for i in range(5):
        fin[2 * i : 2 * i + 1, :] = s[i : i + 1]
        fin[2 * i + 1 : 2 * i + 2, :] = s[8 + i : 9 + i]
    result = jnp.where(lax.rem(x, 2) == 0, fin[0:9, :], fin[1:10, :])
    for i in range(9):
        kg_ref[128 * i : 128 * i + 128] = result[i]
    for is_self, rc in zc:
        @pl.when(jnp.logical_not(is_self))
        def _():
            rc.wait_send()


def closing(enc_in, ing_in, kg_in, enc_out, ing_out, kg_out, sem):
    copies = [
        pltpu.make_async_copy(src, dst, sem.at[i])
        for i, (src, dst) in enumerate(((ing_in, ing_out), (enc_in, enc_out), (kg_in, kg_out)))
    ]
    for c in copies:
        c.start()
    for c in copies:
        c.wait()


def body(snapshots, first_kernel, second_kernel, cotangent):
    def vm(shape, kind=BF):
        return pltpu.VMEM(shape, kind)

    dma = pltpu.SemaphoreType.DMA
    scratch = [
        vm((33, 128, 256)), vm((3, 2, 17, 64, 256)), vm((40, 256), F32), vm((16, 256)), vm((32, 256)), vm((16, 256)),
        vm((9, 256, 256)), vm((9, 256, 256)), vm((24, 64, 256)), vm((3, 24, 64, 256)),
        vm((64, 256), F32), vm((32, 256)), vm((96, 256)), vm((64, 256)), vm((64, 256)),
        vm((24, 80, 256), F32), vm((16, 64, 256)),
        vm((3, 16, 64, 256)), vm((512, 256), F32), vm((128, 1024)), vm((9, 128, 256), F32),
        vm((4, 256, 256), F32), vm((8, 32, 256), F32), vm((4, 256, 256)), vm((3, 256, 256)),
        vm((8, 32, 256), F32), vm((8, 32, 256)), vm((7, 32, 256)), vm((8, 32, 256)), vm((7, 32, 256)),
        vm((4, 16, 256), F32), vm((4, 16, 256)), vm((3, 16, 256)),
        vm((5, 8, 256), F32), vm((80, 256), F32), vm((16, 16, 128)), vm((16, 16, 128)), vm((16, 128), F32),
        vm((9, 64, 256)), vm((9, 64, 256)), vm((9, 80, 256), F32), vm((16, 256)), vm((16, 256)), vm((16, 256)),
        dma((4,)), dma((6,)), dma((6,)), dma((6,)), dma((6,)), dma((6,)), dma((6,)), dma((20,)), dma((20,)),
        dma((15,)), dma((15,)), dma((14,)), dma((14,)), dma((16,)), dma((16,)),
    ]
    enc, ing, kg = pl.pallas_call(
        kernel,
        name="section",
        out_shape=(
            pltpu.VMEM((8, 64, 256), BF),
            pltpu.VMEM((16, 128, 256), BF),
            pltpu.VMEM((1152,), F32),
        ),
        in_specs=[pl.BlockSpec(memory_space=pl.ANY)] * 4,
        out_specs=[pl.BlockSpec(memory_space=pltpu.VMEM)] * 3,
        scratch_shapes=scratch,
        compiler_params=pltpu.CompilerParams(
            collective_id=0, has_side_effects=True, vmem_limit_bytes=56 << 20
        ),
    )(
        snapshots[0],
        jnp.swapaxes(first_kernel, 1, 2),
        jnp.swapaxes(second_kernel, 1, 2),
        cotangent[0],
    )
    enc, ing, kg = pl.pallas_call(
        closing,
        name="closing",
        out_shape=(
            jax.ShapeDtypeStruct((8, 64, 256), BF),
            jax.ShapeDtypeStruct((16, 128, 256), BF),
            jax.ShapeDtypeStruct((1152,), F32),
        ),
        in_specs=[pl.BlockSpec(memory_space=pl.ANY)] * 3,
        out_specs=[pl.BlockSpec(memory_space=pl.ANY)] * 3,
        scratch_shapes=[dma((3,))],
        compiler_params=pltpu.CompilerParams(vmem_limit_bytes=1 << 20),
    )(enc, ing, kg)
    return enc[None], ing[None], kg


def solution(mesh):
    return jax.shard_map(
        body,
        mesh=mesh,
        in_specs=(
            P("batch", "azi", "rad", None),
            P(None, None, "batch"),
            P(None, None, "batch"),
            P("batch", "azi", "rad", None),
        ),
        out_specs=(
            P("batch", "azi", "rad", None),
            P("batch", "azi", "rad", None),
            P(("azi", "rad", "batch")),
        ),
        check_vma=False,
    )
```

```python
import jax
import jax.numpy as jnp
from jax import lax
from jax.experimental import pallas as pl
from jax.experimental.pallas import tpu as pltpu
from jax.sharding import PartitionSpec as P

BF = jnp.bfloat16
F32 = jnp.float32
SHIFTS = (4, 0, -4)


def dot_nt(a, b):
    return lax.dot_general(a, b, (((1,), (1,)), ((), ())), preferred_element_type=F32)


def dot_nn(a, b):
    return lax.dot_general(a, b, (((1,), (0,)), ((), ())), preferred_element_type=F32)


def kernel(
    snap_hbm, w1_hbm, w2_hbm, cot_hbm,
    enc_ref, ing_ref, kg_ref,
    snap, xs, colf, cols_s, cols_r, cols_c, w1, w2, cot24, cot_sh, edgef, cedge_s, cedge_r, aedge_s, aedge_r,
    extf, actr, act_sh, pre, at, gt, g1, g2, xbuf1, xr1, s1, ybuf1, yr1, ybuf2, yr2, s2, xbuf2, xr2,
    zcom, zsum, pbuf, prec, fin, gp, gp1, gpf, gcol_s, gcol_r, gcol_c,
    loc_sem, wsend, wrecv, wfs, wfr, wzs, wzr, hs, hr, xss, xrs, yss, yrs, zss, zrs,
):
    a = lax.axis_index("azi")
    rad = lax.axis_index("rad")
    x = lax.axis_index("batch")
    core = lax.rem(a, 2)
    zlo = lax.rem(a // 2, 4)
    y = a // 8

    def dev(azi, r, b):
        return {"azi": azi, "rad": r, "batch": b}

    def signal(target):
        pl.semaphore_signal(barrier, inc=1, device_id=target, device_id_type=pl.DeviceIdType.MESH)

    def remote(src, dst, ss, rs, target):
        return pltpu.make_async_remote_copy(
            src_ref=src, dst_ref=dst, send_sem=ss, recv_sem=rs,
            device_id=target, device_id_type=pl.DeviceIdType.MESH,
        )

    other = dev(a + 1 - 2 * core, rad, x)
    up = dev(lax.rem(a + 63, 64), rad, x)
    down = dev(lax.rem(a + 1, 64), rad, x)
    band = dev(a, 1 - rad, x)
    step = 2 * core - 1
    near = dev(lax.rem(a + 64 + step, 64), rad, x)

    zi = 4 * rad + zlo

    def along_z(by):
        z2 = lax.rem(zi + 8 + by, 8)
        return dev(y * 8 + lax.rem(z2, 4) * 2 + core, z2 // 4, x)

    z_next, z_prev = along_z(1), along_z(-1)

    def across(target):
        return dev(target["azi"], 1 - rad, x)

    x_peers = [dev(a, rad, lax.rem(x + d, 4)) for d in (1, 2, 3)]
    y_peers = [dev(lax.rem(y + d, 8) * 8 + zlo * 2 + core, rad, x) for d in range(1, 8)]
    own_home = zlo == x

    barrier = pltpu.get_barrier_semaphore()
    for target in [other, up, down, band, across(near), across(up), across(down), z_next, z_prev] + x_peers + y_peers:
        signal(target)
    for cs in range(2):
        for zh in range(2):
            for zl in range(4):
                is_self = own_home & (core == cs) & (rad == zh) & (zlo == zl)

                @pl.when(jnp.logical_not(is_self))
                def _():
                    signal(dev((y * 4 + zl) * 2 + cs, zh, zlo))

    def shard_rows(w):
        return w.at[:, pl.ds(pl.multiple_of(64 * x, 64), 64), :]

    def half_rows(w, xi, k):
        return w.at[:, pl.ds(pl.multiple_of(64 * xi + 32 * k, 32), 32), :]

    own_snap = pl.ds(1 + 16 * core, 16)
    lsnap = pltpu.make_async_copy(snap_hbm, snap.at[own_snap], loc_sem.at[0])
    lw1 = pltpu.make_async_copy(w1_hbm, shard_rows(w1), loc_sem.at[1])
    lw2 = pltpu.make_async_copy(w2_hbm, shard_rows(w2), loc_sem.at[2])
    own_rows = pl.ds(4 + 8 * core, 8)
    lcot = pltpu.make_async_copy(cot_hbm, cot24.at[own_rows], loc_sem.at[3])
    for c in (lcot, lsnap, lw1, lw2):
        c.start()

    def edge(tile_of, out, r):
        low = tile_of(0).astype(F32)[0:4]
        high = tile_of(48).astype(F32)[12:16]
        out[4 * r : 4 * r + 4, :] = jnp.where(rad == 0, high, low)

    lcot.wait()
    for r in range(8):
        edge(lambda c: cot24[4 + 8 * core + r, c : c + 16, :], edgef, r)
    cedge_s[...] = edgef[0:32, :].astype(BF)
    pl.semaphore_wait(barrier, jnp.where(own_home, 34, 35))

    base = pl.ds(pl.multiple_of(32 * core, 32), 32)

    def part_of(w, xi, taps, k):
        return w.at[taps, pl.ds(pl.multiple_of(64 * xi + 32 * k, 32), 32), :]

    def gather_send(w, w_hbm, taps, at_sem):
        out = {}
        for d in (0, 2, 1):
            out[d] = remote(
                w_hbm.at[taps, base, :], part_of(w, x, taps, core), wsend.at[at_sem + d], wrecv.at[at_sem + d], x_peers[d]
            )
            out[d].start()
        return out

    def hand_on(w, d, taps, at_sem):
        part = part_of(w, lax.rem(x + 3 - d, 4), taps, core)
        c = remote(part, part, wfs.at[at_sem + d], wfr.at[at_sem + d], other)
        c.start()
        return c

    every = pl.ds(0, 9)
    g1s = gather_send(w1, w1_hbm, every, 0)
    hsnap = remote(snap_hbm, snap.at[own_snap], hs.at[0], hr.at[0], other)
    hsnap.start()
    row_near = remote(snap_hbm.at[15], snap.at[0], hs.at[6], hr.at[6], near)
    row_pass = remote(snap.at[0], snap.at[0], hs.at[7], hr.at[7], other)

    @pl.when(core == 1)
    def _():
        row_near.start()

    edge_rows = pl.ds(4 * core, 4)
    far_rows = pl.ds(20 * (1 - core), 4)
    mid = pl.ds(pl.multiple_of(16 + 32 * core, 16), 32)
    tip = pl.ds(pl.multiple_of(80 * (1 - core), 16), 16)
    tip_s = pl.ds(pl.multiple_of(16 * core, 16), 16)
    cot_halo = [
        remote(cot_hbm.at[edge_rows], cot24.at[far_rows], hs.at[1], hr.at[1], near),
        remote(cedge_s, cedge_r.at[mid], hs.at[12], hr.at[12], band),
        remote(cedge_s.at[tip_s], cedge_r.at[tip], hs.at[14], hr.at[14], across(near)),
        remote(cot_hbm, cot24.at[own_rows], hs.at[4], hr.at[4], other),
    ]
    for c in cot_halo:
        c.start()
    got_rows = cot24.at[pl.ds(20 * core, 4)]
    got_tip = cedge_r.at[pl.ds(pl.multiple_of(80 * core, 16), 16)]
    cot_pass = [
        remote(got_rows, got_rows, hs.at[2], hr.at[2], other),
        remote(cedge_r.at[mid], cedge_r.at[mid], hs.at[13], hr.at[13], other),
        remote(got_tip, got_tip, hs.at[15], hr.at[15], other),
    ]

    row_i = lax.broadcasted_iota(jnp.int32, (192, 128), 0)
    col_i = lax.broadcasted_iota(jnp.int32, (192, 128), 1)
    pick = jnp.where(col_i == 2 * lax.rem(row_i, 64) + row_i // 64 - 1, 1.0, 0.0).astype(BF)

    lsnap.wait()
    for r in range(16):
        e = 16 * core + 1 + r
        got = dot_nn(pick, snap[e])
        for n in range(3):
            xs[n, (1 + r) % 2, 8 * core + (1 + r) // 2] = got[64 * n : 64 * n + 64].astype(BF)
        colf[r : r + 1, :] = got[191:192]
    cols_s[...] = colf[0:16, :].astype(BF)
    col_rows = pl.ds(pl.multiple_of(16 * core, 16), 16)
    hcols = remote(cols_s, cols_r.at[col_rows], hs.at[3], hr.at[3], band)
    hcols.start()
    cols_pass = remote(cols_r.at[col_rows], cols_r.at[col_rows], hs.at[5], hr.at[5], other)
    tip_near = remote(cols_s, cols_c, hs.at[8], hr.at[8], across(near))
    tip_pass = remote(cols_c, cols_c, hs.at[18], hr.at[18], other)

    @pl.when(core == 1)
    def _():
        tip_near.start()

    hsnap.wait()
    for r in range(16):
        e = 16 * (1 - core) + 1 + r
        got = dot_nn(pick, snap[e])
        for n in range(3):
            xs[n, (1 + r) % 2, 8 * (1 - core) + (1 + r) // 2] = got[64 * n : 64 * n + 64].astype(BF)
    for d in (0, 2, 1):
        g1s[d].wait_recv()
    even = lax.rem(zlo, 2)

    def quarter(w, xi, taps):
        return w.at[taps, pl.ds(pl.multiple_of(64 * xi + 32 * core + 16 * even, 16), 16), :]

    g2s = {}
    for d in (0, 2, 1):
        g2s[d] = remote(
            w2_hbm.at[every, pl.ds(pl.multiple_of(32 * core + 16 * even, 16), 16), :],
            quarter(w2, x, every), wsend.at[3 + d], wrecv.at[3 + d], x_peers[d],
        )
        g2s[d].start()

    @pl.when(core == 0)
    def _():
        row_near.wait_recv()
        row_pass.start()
        tip_near.wait_recv()
        tip_pass.start()

    hcols.wait()
    cols_pass.start()
    for i in range(3):
        cot_halo[i].wait_recv()
        cot_pass[i].start()
    f1 = []
    for d in (0, 2, 1):
        f1.append(hand_on(w1, d, every, 0))

    @pl.when(core == 1)
    def _():
        row_pass.wait_recv()
        tip_pass.wait_recv()
        row_near.wait_send()
        tip_near.wait_send()

    got = dot_nn(pick, snap[0])
    for n in range(3):
        xs[n, 0, 0] = got[64 * n : 64 * n + 64].astype(BF)
    cols_pass.wait()
    in_row = lax.broadcasted_iota(jnp.int32, (16, 256), 0)
    colv = jnp.where(rad == 1, cols_r[...].astype(F32), 0.0)
    corner = jnp.where(rad == 1, cols_c[...].astype(F32), 0.0)
    for e in range(33):
        tile = xs[0, e % 2, e // 2, 0:16, :].astype(F32)
        side = colv[e - 1 : e] if e else corner[15:16]
        xs[0, e % 2, e // 2, 0:16, :] = jnp.where(in_row == 0, side, tile).astype(BF)
    lw1.wait()

    def edges(field, out):
        for r in range(16):
            edge(lambda c: field[r, c : c + 16, :], edgef, r)
        out[...] = edgef[...].astype(BF)

    def shifted(field, edge_got, sh):
        got = edge_got[...].astype(F32)
        for r in range(16):
            extf[r, 8:72, :] = field[r].astype(F32)
            part = got[4 * r : 4 * r + 4]
            extf[r, 4:8, :] = jnp.where(rad == 1, part, 0.0)
            extf[r, 72:76, :] = jnp.where(rad == 0, part, 0.0)
            sh[1, r] = field[r]
            sh[2, r] = extf[r, 4:68, :].astype(BF)
            sh[0, r] = extf[r, 12:76, :].astype(BF)

    def conv1(b, _):
        total = jnp.zeros((256, 128), F32)
        for t in range(9):
            m, n = t // 3, t % 3
            win = xs[n, m % 2, pl.ds(4 * b + m // 2, 4)].reshape(256, 256)
            w = jnp.concatenate(
                [w1[t, pl.ds(pl.multiple_of(64 * i + 32 * core, 32), 32), :] for i in range(4)], axis=0
            )
            total = total + dot_nt(win, w)
        sig = 1.0 / (1.0 + jnp.exp(-total))
        at[:, pl.ds(pl.multiple_of(256 * b, 256), 256)] = (total * sig).astype(BF).T
        return 0

    lax.fori_loop(0, 4, conv1, 0, unroll=True)

    for c in cot_pass:
        c.wait()
    cot_halo[3].wait()
    for c in cot_halo[0:3]:
        c.wait_send()
    got = cedge_r[...].astype(F32)
    for r in range(24):
        extf[r, 8:72, :] = cot24[r].astype(F32)
        part = got[4 * r : 4 * r + 4]
        extf[r, 4:8, :] = jnp.where(rad == 1, part, 0.0)
        extf[r, 72:76, :] = jnp.where(rad == 0, part, 0.0)
        for n, start in ((0, 12), (1, 8), (2, 4)):
            cot_sh[n, r] = extf[r, start : start + 64, :].astype(BF)

    def tiles_before(tile, k):
        q = tile // 9
        return sum((u // 4) % 2 == k for u in range(9 * q, tile))

    xc1 = []
    for chunk, taps in enumerate(((0, 1, 2), (3, 4), (5, 6), (7, 8))):
        for t in taps:
            m, n = t // 3, t % 3
            win = cot_sh[n, 8 - 4 * m : 24 - 4 * m].reshape(1024, 256)
            gt[t] = dot_nn(at[...], win) * (1.0 / 512.0)
        for k in range(2):
            @pl.when(core == k)
            def _():
                for tile in range(72 * chunk, 72 * chunk + 72):
                    if (tile // 4) % 2 != k:
                        continue
                    q, c = tile // 9, tiles_before(tile, k)
                    t, within = tile // 32, tile % 32
                    i = 4 * (within // 8) + within % 4
                    rows = gt[t, 8 * i : 8 * i + 8, :]
                    if c < 4:
                        g1[q % 4, 32 * (q // 4) + 8 * c : 32 * (q // 4) + 8 * c + 8, :] = rows
                    else:
                        g2[q // 4, 8 * (q % 4) : 8 * (q % 4) + 8, :] = rows
                for q in range(8 * chunk, 8 * chunk + 8):
                    if sum((u // 4) % 2 == k for u in range(9 * q, 9 * q + 9)) < 5:
                        g2[q // 4, 8 * (q % 4) : 8 * (q % 4) + 8, :] = jnp.zeros((8, 256), F32)

        some = slice(64 * chunk, 64 * chunk + 64)
        for i in range(4):
            xbuf1[i, some, :] = g1[i, some, :].astype(BF)
        for d in (1, 0, 2):
            c = remote(
                xbuf1.at[lax.rem(x + 1 + d, 4), pl.ds(64 * chunk, 64)], xr1.at[d, pl.ds(64 * chunk, 64)],
                xss.at[3 * chunk + d], xrs.at[3 * chunk + d], x_peers[d],
            )
            c.start()
            xc1.append(c)
    for i in range(8):
        ybuf2[i] = g2[i].astype(BF)
    yc2 = []
    for d in (3, 2, 4, 1, 5, 0, 6):
        c = remote(ybuf2.at[lax.rem(y + 1 + d, 8)], yr2.at[d], yss.at[d], yrs.at[d], y_peers[d])
        c.start()
        yc2.append(c)

    by_z = []
    for d in (0, 2, 1):
        g2s[d].wait_recv()
        for i, (taps, target) in enumerate(((pl.ds(0, 5), z_next), (pl.ds(5, 4), z_prev))):
            part = quarter(w2, lax.rem(x + 3 - d, 4), taps)
            c = remote(part, part, wzs.at[2 * d + i], wzr.at[2 * d + i], target)
            c.start()
            by_z.append(c)

    for c in f1:
        c.wait()
    for d in range(3):
        g1s[d].wait_send()

    def own(b, _):
        at_row = 4 * b
        total = jnp.zeros((256, 256), F32)
        for t in range(9):
            m, n = t // 3, t % 3
            win = xs[n, m % 2, pl.ds(8 * core + at_row + m // 2, 4)].reshape(256, 256)
            total = total + dot_nt(win, w1[t])
        pre[pl.ds(pl.multiple_of(256 * b, 256), 256), :] = total
        sig = 1.0 / (1.0 + jnp.exp(-total))
        actr[pl.ds(4 + at_row, 4)] = (total * sig).astype(BF).reshape(4, 64, 256)
        return 0

    lax.fori_loop(0, 2, own, 0)
    hact_u = remote(actr.at[4:8], actr.at[12:16], hs.at[16], hr.at[16], up)
    hact_u.start()
    hact_d = remote(actr.at[8:12], actr.at[0:4], hs.at[19], hr.at[19], down)
    hact_d.start()

    yc1 = []
    def second_on():
        f2 = []
        for i, d in enumerate((0, 2, 1)):
            by_z[2 * i].wait_recv()
            by_z[2 * i + 1].wait_recv()
            f2.append(hand_on(w2, d, every, 3))
        lw2.wait()
        return f2

    for chunk in range(4):
        if chunk == 2:
            f2 = second_on()
        for c in xc1[3 * chunk : 3 * chunk + 3]:
            c.wait()
        for j in (2 * chunk, 2 * chunk + 1):
            rows = slice(32 * j, 32 * j + 32)
            s = g1[x, rows, :]
            for d in range(3):
                s = s + xr1[d, rows, :].astype(F32)
            s1[j] = s
            ybuf1[j] = s.astype(BF)
            d = lax.rem(j + 7 - y + 8, 8)

            @pl.when(y != j)
            def _():
                remote(
                    ybuf1.at[j], yr1.at[d], yss.at[7 + d], yrs.at[7 + d], dev(j * 8 + zlo * 2 + core, rad, x)
                ).start()
    for d in range(7):
        yc1.append(remote(ybuf1.at[0], yr1.at[d], yss.at[7 + d], yrs.at[7 + d], y_peers[d]))
    for c in yc2:
        c.wait()
    s = g2[y]
    for d in range(7):
        s = s + yr2[d].astype(F32)
    for i in range(4):
        s2[i, 0:8, :] = s[8 * i : 8 * i + 8]
        s2[i, 8:16, :] = jnp.zeros((8, 256), F32)
    for i in range(4):
        xbuf2[i] = s2[i].astype(BF)
    xc2 = []
    for d in (1, 0, 2):
        c = remote(xbuf2.at[lax.rem(x + 1 + d, 4)], xr2.at[d], xss.at[12 + d], xrs.at[12 + d], x_peers[d])
        c.start()
        xc2.append(c)

    hact_d.wait()
    hact_u.wait()
    edges(actr, aedge_s)
    haedge = remote(aedge_s, aedge_r, hs.at[9], hr.at[9], band)
    haedge.start()
    for d in range(3):
        f2[d].wait()
        g2s[d].wait_send()
        by_z[2 * d].wait_send()
        by_z[2 * d + 1].wait_send()

    def back(b, _):
        at_row = 4 * b
        cells = pl.ds(pl.multiple_of(256 * b, 256), 256)
        total = cot24[pl.ds(4 + 8 * core + at_row, 4)].reshape(256, 256).astype(F32)
        for t in range(9):
            m, n = t // 3, t % 3
            win = cot_sh[n, pl.ds(8 * core + at_row + 8 - 4 * m, 4)].reshape(256, 256)
            total = total + dot_nn(win, w2[t])
        v = pre[cells, :]
        s = 1.0 / (1.0 + jnp.exp(-v))
        g = (total * (s * (1.0 + v * (1.0 - s)))).astype(BF)
        gp[pl.ds(at_row, 4)] = g.reshape(4, 64, 256)
        for i in range(4):
            colf[pl.ds(at_row + i, 1), :] = g[64 * i : 64 * i + 16].astype(F32)[0:1]
        return 0

    lax.fori_loop(0, 2, back, 0)
    gcol_s[...] = colf[0:16, :].astype(BF)
    hgp = [
        remote(gp.at[0], gp.at[8], hs.at[10], hr.at[10], up),
        remote(gcol_s, gcol_r, hs.at[11], hr.at[11], band),
        remote(gcol_s, gcol_c, hs.at[17], hr.at[17], across(up)),
    ]
    for c in hgp:
        c.start()

    for c in xc2:
        c.wait()
    s = s2[x]
    for d in range(3):
        s = s + xr2[d].astype(F32)
    zcom[4] = s[0:8]
    for c in yc1:
        c.wait()
    s = s1[y]
    for d in range(7):
        s = s + yr1[d].astype(F32)
    for i in range(4):
        zcom[i] = s[8 * i : 8 * i + 8]
    phase = lax.rem(4 * y + x, 8)
    before = 0
    for u in range(9):
        held = lax.rem((phase + u) // 4, 2) == core
        tile = zcom[before if u == 0 else jnp.minimum(before, 4)]
        zsum[8 * u : 8 * u + 8, :] = jnp.where(held, tile, 0.0)
        before = before + jnp.where(held, 1, 0)
    zsum[72:80, :] = jnp.zeros((8, 256), F32)
    for p in range(16):
        rows = zsum[(9 * p) // 2 : (9 * p) // 2 + 8, :]
        pbuf[p] = jnp.concatenate([rows[:, 0:128], rows[:, 128:256]], axis=0).astype(BF)
    slot = core * 8 + rad * 4 + zlo
    zc = []
    for p in range(16):
        c1, zh, xp = p // 8, (p // 4) % 2, p % 4
        is_self = own_home & (core == c1) & (rad == zh) & (x == xp)
        rc = remote(pbuf.at[p], prec.at[slot], zss.at[p], zrs.at[slot], dev((y * 4 + x) * 2 + c1, zh, xp))
        lc = pltpu.make_async_copy(pbuf.at[p], prec.at[slot], zrs.at[slot])

        @pl.when(is_self)
        def _():
            lc.start()

        @pl.when(jnp.logical_not(is_self))
        def _():
            rc.start()

        zc.append((is_self, rc))

    haedge.wait()
    shifted(actr, aedge_r, act_sh)

    def ahead(b, _):
        at_row = 4 * b
        total = act_sh[1, pl.ds(4 + at_row, 4)].reshape(256, 256).astype(F32)
        for t in range(9):
            m, n = t // 3, t % 3
            win = act_sh[2 - n, pl.ds(at_row + 4 * m, 4)].reshape(256, 256)
            total = total + dot_nt(win, w2[t])
        enc_ref[pl.ds(at_row, 4)] = total.astype(BF).reshape(4, 64, 256)
        return 0

    lax.fori_loop(0, 2, ahead, 0)
    for c in hgp:
        c.wait()
    colv = jnp.where(rad == 0, gcol_r[...].astype(F32), 0.0)
    corner = jnp.where(rad == 0, gcol_c[...].astype(F32), 0.0)
    for r in range(9):
        gpf[r, 0:64, :] = gp[r].astype(F32)
        gpf[r, 64:65, :] = colv[r : r + 1] if r < 8 else corner[0:1]
        gp1[r] = gpf[r, 1:65, :].astype(BF)

    row_q = lax.broadcasted_iota(jnp.int32, (128, 128), 0)
    col_q = lax.broadcasted_iota(jnp.int32, (128, 128), 1)
    weave = jnp.where(col_q == lax.rem(row_q, 2) * 64 + row_q // 2, 1.0, 0.0).astype(BF)
    ptaps = (((1, 0),), ((2, 0), (0, 1)))

    def inward(b, _):
        at_row = 4 * b
        for rp in range(2):
            halves = []
            for cp in range(2):
                total = jnp.zeros((256, 256), F32)
                for m, rs in ptaps[rp]:
                    for n, cs in ptaps[cp]:
                        field = gp1 if cs else gp
                        win = field[pl.ds(at_row + rs, 4)].reshape(256, 256)
                        total = total + dot_nn(win, w1[3 * m + n])
                halves.append(total.astype(BF).reshape(4, 64, 256))
            for i in range(4):
                pair = jnp.concatenate([halves[0][i], halves[1][i]], axis=0)
                ing_ref[2 * (at_row + i) + rp] = dot_nn(weave, pair).astype(BF)
        return 0

    lax.fori_loop(0, 2, inward, 0)

    @pl.when(core == 0)
    def _():
        row_pass.wait_send()
        tip_pass.wait_send()


    for s in range(16):
        pltpu.make_async_copy(pbuf.at[0], prec.at[s], zrs.at[s]).wait()
    s = prec[0].astype(F32)
    for i in range(1, 16):
        s = s + prec[i].astype(F32)
    for i in range(5):
        fin[2 * i : 2 * i + 1, :] = s[i : i + 1]
        fin[2 * i + 1 : 2 * i + 2, :] = s[8 + i : 9 + i]
    result = jnp.where(lax.rem(x, 2) == 0, fin[0:9, :], fin[1:10, :])
    for i in range(9):
        kg_ref[128 * i : 128 * i + 128] = result[i]
    for is_self, rc in zc:
        @pl.when(jnp.logical_not(is_self))
        def _():
            rc.wait_send()


def closing(enc_in, ing_in, kg_in, enc_out, ing_out, kg_out, sem):
    copies = [
        pltpu.make_async_copy(src, dst, sem.at[i])
        for i, (src, dst) in enumerate(((ing_in, ing_out), (enc_in, enc_out), (kg_in, kg_out)))
    ]
    for c in copies:
        c.start()
    for c in copies:
        c.wait()


def body(snapshots, first_kernel, second_kernel, cotangent):
    def vm(shape, kind=BF):
        return pltpu.VMEM(shape, kind)

    dma = pltpu.SemaphoreType.DMA
    scratch = [
        vm((33, 128, 256)), vm((3, 2, 17, 64, 256)), vm((40, 256), F32), vm((16, 256)), vm((32, 256)), vm((16, 256)),
        vm((9, 256, 256)), vm((9, 256, 256)), vm((24, 64, 256)), vm((3, 24, 64, 256)),
        vm((64, 256), F32), vm((32, 256)), vm((96, 256)), vm((64, 256)), vm((64, 256)),
        vm((24, 80, 256), F32), vm((16, 64, 256)),
        vm((3, 16, 64, 256)), vm((512, 256), F32), vm((128, 1024)), vm((9, 128, 256), F32),
        vm((4, 256, 256), F32), vm((8, 32, 256), F32), vm((4, 256, 256)), vm((3, 256, 256)),
        vm((8, 32, 256), F32), vm((8, 32, 256)), vm((7, 32, 256)), vm((8, 32, 256)), vm((7, 32, 256)),
        vm((4, 16, 256), F32), vm((4, 16, 256)), vm((3, 16, 256)),
        vm((5, 8, 256), F32), vm((80, 256), F32), vm((16, 16, 128)), vm((16, 16, 128)), vm((16, 128), F32),
        vm((9, 64, 256)), vm((9, 64, 256)), vm((9, 80, 256), F32), vm((16, 256)), vm((16, 256)), vm((16, 256)),
        dma((4,)), dma((6,)), dma((6,)), dma((6,)), dma((6,)), dma((6,)), dma((6,)), dma((20,)), dma((20,)),
        dma((15,)), dma((15,)), dma((14,)), dma((14,)), dma((16,)), dma((16,)),
    ]
    enc, ing, kg = pl.pallas_call(
        kernel,
        name="section",
        out_shape=(
            pltpu.VMEM((8, 64, 256), BF),
            pltpu.VMEM((16, 128, 256), BF),
            pltpu.VMEM((1152,), F32),
        ),
        in_specs=[pl.BlockSpec(memory_space=pl.ANY)] * 4,
        out_specs=[pl.BlockSpec(memory_space=pltpu.VMEM)] * 3,
        scratch_shapes=scratch,
        compiler_params=pltpu.CompilerParams(
            collective_id=0, has_side_effects=True, vmem_limit_bytes=56 << 20
        ),
    )(
        snapshots[0],
        jnp.swapaxes(first_kernel, 1, 2),
        jnp.swapaxes(second_kernel, 1, 2),
        cotangent[0],
    )
    enc, ing, kg = pl.pallas_call(
        closing,
        name="closing",
        out_shape=(
            jax.ShapeDtypeStruct((8, 64, 256), BF),
            jax.ShapeDtypeStruct((16, 128, 256), BF),
            jax.ShapeDtypeStruct((1152,), F32),
        ),
        in_specs=[pl.BlockSpec(memory_space=pl.ANY)] * 3,
        out_specs=[pl.BlockSpec(memory_space=pl.ANY)] * 3,
        scratch_shapes=[dma((3,))],
        compiler_params=pltpu.CompilerParams(vmem_limit_bytes=1 << 20),
    )(enc, ing, kg)
    return enc[None], ing[None], kg


def solution(mesh):
    return jax.shard_map(
        body,
        mesh=mesh,
        in_specs=(
            P("batch", "azi", "rad", None),
            P(None, None, "batch"),
            P(None, None, "batch"),
            P("batch", "azi", "rad", None),
        ),
        out_specs=(
            P("batch", "azi", "rad", None),
            P("batch", "azi", "rad", None),
            P(("azi", "rad", "batch")),
        ),
        check_vma=False,
    )
```
